128 devices in a mesh: grp: 8 (over y, core), dp: 16 (over x, z).
Axes of the slice: x: 4, y: 4, z: 4, core: 2. Of those that a mesh axis runs over, the one named last changes fastest.
Arguments:
- query_lat: bfloat16 [256, 32, 64, 512], P(('grp', 'dp')), parts along dimension 0, may hold values from -6 to 6
- query_rope: bfloat16 [256, 32, 4096], P(('grp', 'dp')), parts along dimension 0, may hold values from -400 to 400
- lat_cache: bfloat16 [256, 2048, 512], P(('grp', 'dp')), parts along dimension 0, may hold values from -40 to 40
- rope_cache: bfloat16 [256, 64, 2048], P(('grp', 'dp')), parts along dimension 0, may hold values from -8 to 8
- new_lat: bfloat16 [256, 32, 512], P(('grp', 'dp')), parts along dimension 0, may hold values from -6 to 6
- new_rope: bfloat16 [256, 32, 64], P(('grp', 'dp')), parts along dimension 0, may hold values from -6 to 6
- cache_len: int32 [256], P(('grp', 'dp')), parts along dimension 0, may hold values from 2 to 2048, as said below
- live_rows: int32 [256], P(('grp', 'dp')), parts along dimension 0, may hold values from 1 to 32, as said below
- ancestors: int32 [256, 32, 32], P(('grp', 'dp')), parts along dimension 0, may hold values from 0 to 1, as said below
- value_up: bfloat16 [64, 512, 128], P('dp'), may hold values from -0.25 to 0.25
- out_proj: bfloat16 [8192, 7168], P('dp'), may hold values from -0.0625 to 0.0625
Outputs:
- attn_out: bfloat16 [8192, 7168], P(('grp', 'dp')), parts along dimension 0
The draws below stay inside these ranges and needn't reach their ends.
There are 8 independent parts, one for each index of `grp`. The reference program is written for one: setup_inputs(seed, part) draws one part's arguments, and reference() takes and returns one part's arrays. A program takes and returns all parts, laid end to end along the dimension named above; an argument that names none is the same for every part. Nothing has to cross between parts.
Inputs may be any that keep to these rules, and one draw needn't show every extreme that they name: `cache_len`: at least 2; the largest equals 2048 in every draw. `live_rows`: the largest equals 32 in every draw. ancestors[r, i, j] is 1 exactly when tree row j is row i or an ancestor of it; row 0 is the root and every ancestor of row i has a smaller index.
All inputs are finite; a program needn't handle non-finite values.
Results may differ from the reference program's by a relative error of at most 0.02.
Values may be sent and summed in bfloat16 or wider, within the bound.
A program may use at most 128 MiB of HBM per device.

```python
import jax
import jax.numpy as jnp
from jax import lax

H = 64
DL = 512
DR = 64
VD = 128
D = 7168
W = 32
REQ_DEV = 2
LMAX = 2048
REQS = 32
ROWS = 1024
N_DP = 16


def rope_base(key):
    base_key = jax.random.fold_in(key, 101)
    return jax.random.normal(base_key, (REQS, LMAX, DR), jnp.float32)


def draw_query_rope(key, part):
    key = jax.random.fold_in(key, 4)
    queries = jax.random.normal(key, (REQS, W, H, DR), jnp.float32)
    return queries.reshape(REQS, W, H * DR).astype(jnp.bfloat16)


def draw_rope_cache(key, part):
    base = rope_base(key)
    return jnp.transpose(base, (0, 2, 1)).astype(jnp.bfloat16)


def draw_lat_cache(key, part):
    key = jax.random.fold_in(key, 5)
    first_key = jax.random.fold_in(key, 0)
    latents = jax.random.normal(first_key, (REQS, LMAX, DL), jnp.float32)
    return latents.astype(jnp.bfloat16)


def draw_cache_len(key, part):
    key = jax.random.fold_in(key, 7)
    first_key, second_key, third_key = jax.random.split(key, 3)
    base = jax.random.randint(first_key, (REQS,), 2, LMAX + 1)
    levels = jax.random.randint(second_key, (REQS // REQ_DEV,), 1, 5)
    levels = jnp.repeat(levels, REQ_DEV)
    lengths = jnp.maximum(2, base * levels // 4)
    chosen = jax.random.randint(third_key, (), 0, REQS)
    return lengths.at[chosen].set(LMAX).astype(jnp.int32)


def draw_live_rows(key, part):
    key = jax.random.fold_in(key, 8)
    first_key, second_key = jax.random.split(key)
    counts = jax.random.randint(first_key, (REQS,), 1, W + 1)
    chosen = jax.random.randint(second_key, (), 0, REQS)
    return counts.at[chosen].set(W).astype(jnp.int32)


def draw_ancestors(key, part):
    key = jax.random.fold_in(key, 9)
    raw_draw = jax.random.randint(key, (REQS, W), 0, W)
    positions = jnp.arange(W, dtype=jnp.int32)
    parents = raw_draw % jnp.maximum(positions, 1)[None, :]
    eye_rows = jnp.eye(W, dtype=jnp.int32)
    result = jnp.broadcast_to(eye_rows, (REQS, W, W))
    for row_index in range(1, W):
        picker = parents[:, row_index][:, None, None] * jnp.ones((1, 1, W), jnp.int32)
        parent_rows = jnp.take_along_axis(result, picker, axis=1)[:, 0]
        result = result.at[:, row_index].set(jnp.maximum(parent_rows, eye_rows[row_index][None, :]))
    return result.astype(jnp.int32)


def block_scale(rng, shape, cuts, smallest, high):
    loudness, own = 1.0, jax.random.fold_in(rng, 6)
    for axis_at, blocks in cuts:
        heights = jnp.exp(jax.random.uniform(jax.random.fold_in(own, axis_at), (blocks,), jnp.float32, smallest / len(cuts), high / len(cuts)))
        loudness = loudness * jnp.repeat(heights, shape[axis_at] // blocks).reshape([-1 if axis == axis_at else 1 for axis in range(len(shape))])
    return loudness


def gaussian(rng, shape, deviation, most, cuts=(), kind=jnp.bfloat16):
    loudness = block_scale(rng, shape, cuts, -0.22, 0.18) if cuts else 1.0
    drawn = jax.random.normal(rng, shape, jnp.float32) * deviation * loudness
    return jnp.minimum(jnp.maximum(drawn, -most), most).astype(kind)


def setup_inputs(seed: int = 0, part: int = 0) -> dict:
    keys = jax.random.split(jax.random.key(seed), 12)
    part_keys = jax.random.split(jax.random.fold_in(keys[11], part), 12)
    query_lat = gaussian(part_keys[0], (REQS, W, H, DL), 1.0, 6.0, ((0, 16),))
    query_rope = draw_query_rope(jax.random.fold_in(jax.random.fold_in(keys[11], part), 71), part)
    lat_cache = draw_lat_cache(jax.random.fold_in(jax.random.fold_in(keys[11], part), 71), part)
    rope_cache = draw_rope_cache(jax.random.fold_in(jax.random.fold_in(keys[11], part), 71), part)
    new_lat = gaussian(part_keys[4], (REQS, W, DL), 1.0, 6.0, ((0, 16),))
    new_rope = gaussian(part_keys[5], (REQS, W, DR), 1.0, 6.0, ((0, 16),))
    cache_len = draw_cache_len(jax.random.fold_in(jax.random.fold_in(keys[11], part), 71), part)
    live_rows = draw_live_rows(jax.random.fold_in(jax.random.fold_in(keys[11], part), 71), part)
    ancestors = draw_ancestors(jax.random.fold_in(jax.random.fold_in(keys[11], part), 71), part)
    value_up = gaussian(keys[9], (H, DL, VD), DL ** -0.5, 0.25, ((0, 16),))
    out_proj = gaussian(keys[10], (H * VD, D), (H * VD) ** -0.5, 0.0625, ((0, 16),))
    return dict(query_lat=query_lat, query_rope=query_rope, lat_cache=lat_cache, rope_cache=rope_cache, new_lat=new_lat, new_rope=new_rope, cache_len=cache_len, live_rows=live_rows, ancestors=ancestors, value_up=value_up, out_proj=out_proj)


score_scale = 192.0 ** -0.5


def one_request(item):
    query_lat, query_rope, lat_cache, rope_cache, new_lat, new_rope, length, live, ancestors = item
    query_full = query_lat.astype(jnp.float32)
    rope_full = query_rope.astype(jnp.float32).reshape(W, H, DR)
    cache_full = lat_cache.astype(jnp.float32)
    tree_full = new_lat.astype(jnp.float32)
    cache_scores = (jnp.einsum('whc,pc->whp', query_full, cache_full)
                    + jnp.einsum('whr,rp->whp', rope_full, rope_cache.astype(jnp.float32))) * score_scale
    positions = jnp.arange(LMAX, dtype=jnp.int32)
    cache_scores = jnp.where(positions[None, None, :] < length, cache_scores, -jnp.inf)
    tree_scores = (jnp.einsum('whc,jc->whj', query_full, tree_full)
                   + jnp.einsum('whr,jr->whj', rope_full, new_rope.astype(jnp.float32))) * score_scale
    tree_scores = jnp.where(ancestors[:, None, :] > 0, tree_scores, -jnp.inf)
    top = jnp.maximum(jnp.max(cache_scores, axis=-1), jnp.max(tree_scores, axis=-1))
    cache_weights = jnp.exp(cache_scores - top[..., None])
    tree_weights = jnp.exp(tree_scores - top[..., None])
    total = jnp.sum(cache_weights, axis=-1) + jnp.sum(tree_weights, axis=-1)
    cache_probs = cache_weights.astype(jnp.bfloat16).astype(jnp.float32)
    tree_probs = tree_weights.astype(jnp.bfloat16).astype(jnp.float32)
    context = jnp.einsum('whp,pc->whc', cache_probs, cache_full) + jnp.einsum('whj,jc->whc', tree_probs, tree_full)
    context = context / total[..., None]
    alive = jnp.arange(W, dtype=jnp.int32)[:, None, None] < live
    return jnp.where(alive, context, 0.0).astype(jnp.bfloat16)


def reference(query_lat, query_rope, lat_cache, rope_cache, new_lat, new_rope, cache_len, live_rows, ancestors, value_up, out_proj):
    context = lax.map(one_request, (query_lat, query_rope, lat_cache, rope_cache, new_lat, new_rope, cache_len, live_rows, ancestors))
    context = context.reshape(ROWS, H, DL)
    head_values = jnp.einsum('nhc,hcv->nhv', context.astype(jnp.float32), value_up.astype(jnp.float32)).astype(jnp.bfloat16)
    group_heads = H // N_DP
    grouped = jnp.moveaxis(head_values.reshape(ROWS, N_DP, group_heads * VD), 1, 0)
    weights_grouped = out_proj.reshape(N_DP, group_heads * VD, D)

    def add_group(summed, pieces):
        values_group, weight_group = pieces
        partial_term = jnp.dot(values_group, weight_group, preferred_element_type=jnp.float32).astype(jnp.bfloat16)
        partial_term = lax.optimization_barrier(partial_term)
        return summed + partial_term.astype(jnp.float32), None

    summed, unused = lax.scan(add_group, jnp.zeros((ROWS, D), jnp.float32), (grouped, weights_grouped))
    return summed.astype(jnp.bfloat16)
```

```python
import functools
import jax
import jax.numpy as jnp
from jax import lax
from jax.experimental import pallas as pl
from jax.experimental.pallas import tpu as pltpu
from jax.sharding import PartitionSpec as P

score_scale = 192.0 ** (-0.5)
log2_e = 1.4426950408889634
very_negative = -1e30


def attend_kernel(
    rows_blk, key_blk, halves,
    len_ref, live_ref,
    q_ref, qr_ref, lat_ref, rope_ref, new_ref, newr_ref, anc_ref,
    out_ref, top_s, tot_s, acc_s,
):
    request = pl.program_id(0)
    length, live = len_ref[request], live_ref[request]
    heads = q_ref.shape[2]
    width = q_ref.shape[3]
    nrow = rows_blk * heads
    sub = nrow // halves
    sub_rows = rows_blk // halves
    factor = score_scale * log2_e
    nt = (((1,), (1,)), ((), ()))

    def scores_of(queries, ropes, keys, rope_keys):
        s = lax.dot_general(queries, keys, nt, preferred_element_type=jnp.float32)
        s = s + jnp.dot(ropes, rope_keys, preferred_element_type=jnp.float32)
        return s * factor

    def lane_sum(w):
        n = w.shape[1]
        parts = [w[:, c * 128:(c + 1) * 128] for c in range(n // 128)]
        while len(parts) > 1:
            parts = [a + b for a, b in zip(parts[::2], parts[1::2])] + (parts[-1:] if len(parts) % 2 else [])
        return parts[0]

    def queries_of(base, half):
        row0 = base + half * sub_rows
        q = q_ref[0, pl.ds(row0, sub_rows)].reshape(sub, width)
        qr = qr_ref[0, pl.ds(pl.multiple_of(row0 * heads, 8), sub), :]
        return q, qr

    def tree_step(base):
        for half in range(halves):
            q, qr = queries_of(base, half)
            row0 = base + half * sub_rows
            s = lax.dot_general(q, new_ref[0], nt, preferred_element_type=jnp.float32)
            s = s + lax.dot_general(qr, newr_ref[0], nt, preferred_element_type=jnp.float32)
            s = s * factor
            anc = anc_ref[0, pl.ds(row0, sub_rows), :]
            n = anc.shape[1]
            bias = jnp.where(anc > 0, 0.0, very_negative)
            s = (s.reshape(sub_rows, heads, n) + bias[:, None, :]).reshape(sub, n)
            top = jnp.max(s, axis=1, keepdims=True)
            w = jnp.exp2(s - top)
            rows = pl.ds(half * sub, sub)
            top_s[rows, :] = jnp.broadcast_to(top, (sub, 128))
            tot_s[rows, :] = jnp.sum(w, axis=1, keepdims=True) * jnp.where(
                lax.broadcasted_iota(jnp.int32, (1, 128), 1) == 0, 1.0, 0.0)
            acc_s[rows, :] = jnp.dot(w.astype(jnp.bfloat16), new_ref[0], preferred_element_type=jnp.float32)

    def cache_step(base, offset, size, masked):
        keys = lat_ref[0, pl.ds(offset, size), :]
        rope_keys = rope_ref[0, :, pl.ds(offset, size)]
        for half in range(halves):
            q, qr = queries_of(base, half)
            s = scores_of(q, qr, keys, rope_keys)
            if masked:
                position = offset + lax.broadcasted_iota(jnp.int32, (1, size), 1)
                s = jnp.where(position < length, s, very_negative)
            rows = pl.ds(half * sub, sub)
            old = top_s[rows, :]
            new = jnp.maximum(old, jnp.max(s, axis=1, keepdims=True))
            rescale = jnp.exp2(old - new)
            w = jnp.exp2(s - new[:, :1])
            tot_s[rows, :] = tot_s[rows, :] * rescale + lane_sum(w)
            top_s[rows, :] = new
            acc_s[rows, :] = acc_s[rows, :] * rescale[:, :1] + jnp.dot(
                w.astype(jnp.bfloat16), keys, preferred_element_type=jnp.float32)

    full = length // key_blk
    rest = length - full * key_blk
    tail = pl.multiple_of(full * key_blk, key_blk)

    def row_block(index, carry):
        base = index * rows_blk
        tree_step(base)

        def key_step(k, c):
            cache_step(base, pl.multiple_of(k * key_blk, key_blk), key_blk, False)
            return c

        lax.fori_loop(0, full, key_step, 0)

        @pl.when(rest > key_blk // 2)
        def _():
            cache_step(base, tail, key_blk, True)

        @pl.when(jnp.logical_and(rest > 0, rest <= key_blk // 2))
        def _():
            cache_step(base, tail, key_blk // 2, True)

        for half in range(halves):
            rows = pl.ds(half * sub, sub)
            total = jnp.sum(tot_s[rows, :], axis=1, keepdims=True)
            ctx = acc_s[rows, :] * (1.0 / total)
            row0 = base + half * sub_rows
            alive = row0 + lax.broadcasted_iota(jnp.int32, (sub_rows, heads, 1), 0) < live
            ctx = jnp.where(alive, ctx.reshape(sub_rows, heads, width), 0.0)
            out_ref[0, pl.ds(row0, sub_rows)] = ctx.astype(out_ref.dtype)
        return carry

    blocks = (live + rows_blk - 1) // rows_blk
    lax.fori_loop(0, blocks, row_block, 0)

    def clear(index, carry):
        out_ref[0, pl.ds(index * rows_blk, rows_blk)] = jnp.zeros((rows_blk, heads, width), out_ref.dtype)
        return carry

    lax.fori_loop(blocks, q_ref.shape[1] // rows_blk, clear, 0)


def attend(query_lat, query_rope, lat_cache, rope_cache, new_lat, new_rope, cache_len, live_rows, ancestors,
           rows_blk=8, key_blk=512, halves=2):
    reqs, rows, heads, width = query_lat.shape
    ropes = query_rope.reshape(reqs, rows * heads, -1)
    nrow = rows_blk * heads

    def whole(x):
        nd = x.ndim
        return pl.BlockSpec((1,) + x.shape[1:], lambda r, *_: (r,) + (0,) * (nd - 1))

    args = (query_lat, ropes, lat_cache, rope_cache, new_lat, new_rope, ancestors)
    return pl.pallas_call(
        functools.partial(attend_kernel, rows_blk, key_blk, halves),
        grid_spec=pltpu.PrefetchScalarGridSpec(
            num_scalar_prefetch=2,
            grid=(reqs,),
            in_specs=[whole(x) for x in args],
            out_specs=whole(query_lat),
            scratch_shapes=[
                pltpu.VMEM((nrow, 128), jnp.float32),
                pltpu.VMEM((nrow, 128), jnp.float32),
                pltpu.VMEM((nrow, width), jnp.float32),
            ],
        ),
        out_shape=jax.ShapeDtypeStruct(query_lat.shape, jnp.bfloat16),
        compiler_params=pltpu.CompilerParams(vmem_limit_bytes=48 * 2**20),
        cost_estimate=pl.CostEstimate(flops=13 * 10**9, bytes_accessed=14 * 2**20, transcendentals=6 * 2**20),
    )(cache_len, live_rows, *args)


def per_device(query_lat, query_rope, lat_cache, rope_cache, new_lat, new_rope, cache_len, live_rows, ancestors,
               value_up, out_proj):
    all_up = lax.all_gather(value_up, "dp", axis=0, tiled=True)
    context = attend(query_lat, query_rope, lat_cache, rope_cache, new_lat, new_rope, cache_len, live_rows, ancestors)
    reqs, rows, heads, width = context.shape
    context = context.reshape(reqs * rows, heads, width)
    head_values = jnp.einsum("nhc,hcv->nhv", context, all_up, preferred_element_type=jnp.float32).astype(jnp.bfloat16)
    exchanged = lax.all_to_all(head_values, "dp", split_axis=1, concat_axis=0, tiled=True)
    flat_values = exchanged.reshape(exchanged.shape[0], -1)
    return lax.psum_scatter(
        jnp.dot(flat_values, out_proj, preferred_element_type=jnp.float32).astype(jnp.bfloat16),
        "dp", scatter_dimension=0, tiled=True)


def solution(mesh):
    both = ("grp", "dp")
    in_specs = (
        P(both, None, None, None), P(both, None, None), P(both, None, None), P(both, None, None),
        P(both, None, None), P(both, None, None), P(both), P(both), P(both, None, None),
        P("dp", None, None), P("dp", None),
    )
    return jax.shard_map(per_device, mesh=mesh, in_specs=in_specs, out_specs=P(both, None), check_vma=False)
```

```python
import functools
import jax
import jax.numpy as jnp
from jax import lax
from jax.experimental import pallas as pl
from jax.experimental.pallas import tpu as pltpu
from jax.sharding import PartitionSpec as P

score_scale = 192.0 ** (-0.5)
log2_e = 1.4426950408889634
very_negative = -1e30
MESH = pl.DeviceIdType.MESH
nt = (((1,), (1,)), ((), ()))


def nbr(base, step):
    return lax.rem(base + step % 4, 4) if step % 4 else base


class Remote:
    def __init__(self, mover, src, dst, step):
        self.mover, self.src, self.dst, self.step = mover, src, dst, step
        self.number = mover.used
        mover.used += 1
        mover.made.append(self)

    def copy(self):
        m = self.mover
        return pltpu.make_async_remote_copy(
            src_ref=self.src(), dst_ref=self.dst(), send_sem=m.send.at[self.number], recv_sem=m.recv.at[self.number],
            device_id=m.device(**self.step), device_id_type=MESH)

    def start(self):
        self.copy().start()
        return self

    def wait_recv(self):
        self.copy().wait_recv()

    def wait_send(self):
        self.copy().wait_send()


class Mover:
    def __init__(self, send, recv):
        self.send, self.recv, self.used, self.made = send, recv, 0, []
        grp, dp = lax.axis_index("grp"), lax.axis_index("dp")
        self.y, self.c = grp // 2, lax.rem(grp, 2)
        self.x, self.z = dp // 4, lax.rem(dp, 4)

    def device(self, x=0, y=0, z=0, c=0):
        cc = lax.rem(self.c + c, 2) if c else self.c
        return (nbr(self.y, y) * 2 + cc, nbr(self.x, x) * 4 + nbr(self.z, z))

    def greet(self, steps):
        barrier = pltpu.get_barrier_semaphore()
        for step in steps:
            pl.semaphore_signal(barrier, inc=1, device_id=self.device(**step), device_id_type=MESH)
        pl.semaphore_wait(barrier, len(steps))

    def later(self, src, dst, **step):
        return Remote(self, src, dst, step)

    def go(self, src, dst, **step):
        return Remote(self, lambda: src, lambda: dst, step).start()


def gather_plan(m, up_ref, proj_ref, all_ref, blk_ref, up_own, blk_own, local):
    x, y, z, c = m.x, m.y, m.z, m.c
    shard = x * 4 + z
    half = pl.ds(pl.multiple_of(c * 256, 256), 256)
    pq = [pl.ds(pl.multiple_of(c * 256 + i * 128, 128), 128) for i in range(2)]
    column = lambda base: pl.ds(base * 4, 4)
    lower = lambda base: pl.ds(base * 4, 2)
    upper = lambda base: pl.ds(base * 4 + 2, 2)
    xl, xr, xo = nbr(x, -1), nbr(x, 1), nbr(x, 2)
    yl, yr, yo = nbr(y, -1), nbr(y, 1), nbr(y, 2)
    zl, zr, zo = nbr(z, -1), nbr(z, 1), nbr(z, 2)

    def at(ref, *index):
        return lambda: ref.at[index]

    def same(ref, *index, **step):
        view = at(ref, *index)
        return m.later(view, view, **step)

    def cols(h):
        return pl.ds(pl.multiple_of(y * 1792 + h * 896, 128), 896)

    def bounce(i, src, mid, dst):
        return (lambda: pltpu.make_async_copy(src(), mid(), local.at[2 * i]),
                lambda: pltpu.make_async_copy(mid(), dst(), local.at[2 * i + 1]))

    own = [bounce(0, at(up_ref, y, half), lambda: up_own, at(all_ref, shard, y, half))]
    for h in range(2):
        own.append(bounce(1 + h, at(proj_ref, slice(None), cols(h)), at(blk_own, h), at(blk_ref, h, z)))

    twins = {}

    def twin(name, ref, *index):
        twins.setdefault(name, []).append(same(ref, *index, c=1))

    zs = [m.later(at(up_ref, y, half), at(all_ref, shard, y, half), z=s) for s in (1, -1, 2)]
    mine = at(proj_ref, slice(None), pl.ds(pl.multiple_of(y * 1792 + c * 896, 128), 896))
    w = [m.later(mine, at(blk_ref, c, z), z=s) for s in (1, -1)]
    wf = [same(blk_ref, c, zl, pl.ds(0, 256), z=1), same(blk_ref, c, zr, pl.ds(256, 256), z=-1)]
    xp = [same(all_ref, column(x), y, pq[0], x=s) for s in (1, -1)]
    yq = [same(all_ref, column(x), y, pq[1], y=s) for s in (1, -1)]
    xpf = [same(all_ref, lower(xl), y, pq[0], x=1), same(all_ref, upper(xr), y, pq[0], x=-1)]
    yqf = [same(all_ref, lower(x), yl, pq[1], y=1), same(all_ref, upper(x), yr, pq[1], y=-1)]
    bases_x, bases_y = (x, xl, xr, xo), (y, yl, yr, yo)
    yp = [[same(all_ref, column(b), y, pq[0], y=s) for s in (1, -1)] for b in bases_x]
    xq = [[same(all_ref, column(x), b, pq[1], x=s) for s in (1, -1)] for b in bases_y]
    ypf = [[same(all_ref, lower(b), yl, pq[0], y=1), same(all_ref, upper(b), yr, pq[0], y=-1)] for b in bases_x]
    xqf = [[same(all_ref, lower(xl), b, pq[1], x=1), same(all_ref, upper(xr), b, pq[1], x=-1)] for b in bases_y]

    twin("spread", all_ref, column(x), y, half)
    for b in (xl, xr):
        twin("near", all_ref, column(b), y, pq[0])
    for b in (yl, yr):
        twin("near", all_ref, column(x), b, pq[1])
    twin("far", all_ref, column(xo), y, pq[0])
    twin("far", all_ref, column(x), yo, pq[1])
    for k in range(4):
        name = "pass%d" % min(k + 1, 3)
        for b in (yl, yr):
            twin(name, all_ref, column(bases_x[k]), b, pq[0])
        for b in (xl, xr):
            twin(name, all_ref, column(b), bases_y[k], pq[1])
        name = "tail%d" % (k // 2)
        twin(name, all_ref, column(bases_x[k]), yo, pq[0])
        twin(name, all_ref, column(xo), bases_y[k], pq[1])
    twin("weights", blk_ref, c, zl)
    twin("weights", blk_ref, c, zr)
    twin("last", blk_ref, c, zo)

    def start(*copies):
        for copy in copies:
            copy.start()

    def got(*copies):
        for copy in copies:
            copy.wait_recv()

    def first():
        for load, _ in own:
            load().start()
        m.greet([dict(x=1), dict(x=-1), dict(y=1), dict(y=-1), dict(z=1), dict(z=-1), dict(z=2), dict(c=1)])
        start(*zs, *w)
        own[0][0]().wait()
        own[0][1]().start()

    def spread():
        for load, store in own[1:]:
            load().wait()
            store().start()
        own[0][1]().wait()
        got(*zs)
        start(*xp, *yq, *yp[0], *xq[0])
        start(*twins["spread"])

    def near():
        got(*xp)
        start(*xpf)
        got(*yq)
        start(*yqf)
        start(*yp[1], *xq[1])
        start(*twins["near"])

    def far():
        got(*xpf, *yqf)
        got(*yp[0], *xq[0])
        start(*yp[2], *xq[2], *ypf[0], *xqf[0])
        start(*twins["far"])

    def pass_on(k):
        def step():
            got(*yp[k], *xq[k])
            start(*ypf[k], *xqf[k])
            if k == 1:
                start(*yp[3], *xq[3])
            start(*twins["pass%d" % k])
        return step

    def weights():
        got(*w)
        start(*wf)
        start(*twins["weights"])

    def tail(name, ks):
        def step():
            for k in ks:
                got(*ypf[k], *xqf[k])
            start(*twins[name])
        return step

    def last():
        got(*wf)
        start(*twins["last"])
        for group in twins.values():
            got(*group)
        for copy in m.made:
            copy.wait_send()
        for _, store in own[1:]:
            store().wait()

    return dict(first=first, spread=spread, near=near, far=far, pass1=pass_on(1), pass2=pass_on(2), pass3=pass_on(3),
                weights=weights, tail0=tail("tail0", (0, 1)), tail1=tail("tail1", (2, 3)), last=last)


schedule = {0: "spread", 3: "near", 5: "far", 7: "pass1", 9: "pass2", 10: "weights", 11: "pass3", 12: "tail0", 13: "tail1"}


def lane_sum(w):
    parts = [w[:, c * 128:(c + 1) * 128] for c in range(w.shape[1] // 128)]
    while len(parts) > 1:
        parts = [a + b for a, b in zip(parts[::2], parts[1::2])] + (parts[-1:] if len(parts) % 2 else [])
    return parts[0]


def attend_kernel(
    len_ref, live_ref, q_hbm, qr_hbm, lat_hbm, rope_hbm, new_ref, newr_ref, anc_ref, up_ref, proj_ref,
    ctx_hbm, all_ref, blk_ref,
    q_ref, qr_ref, lat_ref, rope_ref, up_own, blk_own, top_s, tot_s, acc_s, turn_s, ctx_s,
    send, recv, local, loads,
):
    factor = score_scale * log2_e
    heads, width, key_blk, sub = 64, 512, 1024, 256
    m = Mover(send, recv)
    plan = gather_plan(m, up_ref, proj_ref, all_ref, blk_ref, up_own, blk_own, local)

    def fetch(r):
        pairs = ((q_hbm.at[r], q_ref.at[r]), (qr_hbm.at[r], qr_ref.at[r]), (lat_hbm.at[r], lat_ref.at[r]),
                 (rope_hbm.at[r], rope_ref.at[r, pl.ds(0, 64)]))
        return [pltpu.make_async_copy(src, dst, loads.at[r * 4 + i]) for i, (src, dst) in enumerate(pairs)]

    def deliver(r):
        rows = pl.ds(r * 32, 32)
        return pltpu.make_async_copy(ctx_s.at[:, rows], ctx_hbm.at[:, rows], loads.at[8 + r])

    for r in range(2):
        for copy in fetch(r):
            copy.start()
    plan["first"]()
    for r in range(2):
        position = lax.broadcasted_iota(jnp.int32, (64, 2048), 1)
        row = lax.broadcasted_iota(jnp.int32, (64, 2048), 0)
        outside = jnp.logical_and(row == 0, position >= len_ref[r])
        rope_ref[r, pl.ds(64, 64), :] = jnp.where(outside, very_negative, 0.0).astype(jnp.bfloat16)

    def step(i, carry):
        for r in range(2):
            @pl.when(i == r * 8)
            def _():
                for copy in fetch(r):
                    copy.wait()

        request = i // 8
        block = lax.rem(i, 8) // 2
        key = lax.rem(i, 2)
        row0 = block * 8

        def queries(part):
            start = pl.multiple_of(row0 * heads + part * sub, sub)
            return q_ref[request, pl.ds(start, sub), :], qr_ref[request, pl.ds(start, sub), :]

        @pl.when(key == 0)
        def _():
            for part in range(2):
                q, qr = queries(part)
                rows = pl.ds(part * sub, sub)
                s = lax.dot_general(q, new_ref[request], nt, preferred_element_type=jnp.float32)
                s = s + lax.dot_general(qr[:, :64], newr_ref[request], nt, preferred_element_type=jnp.float32)
                s = s * factor
                anc = anc_ref[request, pl.ds(row0 + part * 4, 4), :]
                bias = jnp.where(anc > 0, 0.0, very_negative)
                s = (s.reshape(4, heads, 32) + bias[:, None, :]).reshape(sub, 32)
                top = jnp.max(s, axis=1, keepdims=True)
                w = jnp.exp2(s - top)
                top_s[rows, :] = jnp.broadcast_to(top, (sub, 128))
                tot_s[rows, :] = jnp.where(lax.broadcasted_iota(jnp.int32, (sub, 128), 1) == 0,
                                           jnp.sum(w, axis=1, keepdims=True), 0.0)
                acc_s[rows, :] = jnp.dot(w.astype(jnp.bfloat16), new_ref[request], preferred_element_type=jnp.float32)

        offset = pl.multiple_of(key * key_blk, key_blk)
        keys = lat_ref[request, pl.ds(offset, key_blk), :]
        rope_keys = rope_ref[request, :, pl.ds(offset, key_blk)]
        scores = []
        for part in range(2):
            q, qr = queries(part)
            scores.append(lax.dot_general(q, keys, nt, preferred_element_type=jnp.float32)
                          + jnp.dot(qr, rope_keys, preferred_element_type=jnp.float32))
        for part in range(2):
            s = scores[part]
            rows = pl.ds(part * sub, sub)
            old = top_s[rows, :]
            new = jnp.maximum(old, jnp.max(s, axis=1, keepdims=True) * factor)
            rescale = jnp.exp2(old - new)
            w = jnp.exp2(s * factor - new[:, :1])
            tot_s[rows, :] = tot_s[rows, :] * rescale + lane_sum(w)
            top_s[rows, :] = new
            acc_s[rows, :] = acc_s[rows, :] * rescale[:, :1] + jnp.dot(
                w.astype(jnp.bfloat16), keys, preferred_element_type=jnp.float32)

        @pl.when(key == 1)
        def _():
            total = jnp.sum(tot_s[...], axis=1, keepdims=True)
            ctx = (acc_s[...] * (1.0 / total)).reshape(8, heads, width)
            alive = row0 + lax.broadcasted_iota(jnp.int32, (8, heads, 1), 0) < live_ref[request]
            ctx = jnp.where(alive, ctx, 0.0)
            turn_s[:, pl.ds(pl.multiple_of(row0, 8), 8), :] = jnp.swapaxes(ctx, 0, 1)

        for r in range(2):
            @pl.when(i == r * 8 + 7)
            def _():
                ctx_s[:, pl.ds(r * 32, 32), :] = turn_s[...].astype(jnp.bfloat16)
                deliver(r).start()

        for point, name in schedule.items():
            pl.when(i == point)(functools.partial(plan[name]))
        return carry

    lax.fori_loop(0, 16, step, 0)
    plan["last"]()
    for r in range(2):
        deliver(r).wait()


def attend(query_lat, query_rope, lat_cache, rope_cache, new_lat, new_rope, cache_len, live_rows, ancestors,
           value_up, out_proj):
    bf = jnp.bfloat16
    queries = query_lat.reshape(2, 2048, 512)
    ropes = query_rope.reshape(2, 2048, 64)
    ropes = jnp.concatenate([ropes, jnp.ones((2, 2048, 1), bf), jnp.zeros((2, 2048, 63), bf)], axis=2)
    anywhere = pl.BlockSpec(memory_space=pl.ANY)
    smem, vmem = pl.BlockSpec(memory_space=pltpu.SMEM), pl.BlockSpec(memory_space=pltpu.VMEM)
    copies = 96
    return pl.pallas_call(
        attend_kernel,
        out_shape=(
            jax.ShapeDtypeStruct((64, 64, 512), bf),
            jax.ShapeDtypeStruct((16,) + value_up.shape, bf),
            jax.ShapeDtypeStruct((2, 4, 512, 896), bf),
        ),
        in_specs=[smem, smem] + [anywhere] * 4 + [vmem] * 3 + [anywhere] * 2,
        out_specs=[anywhere] * 3,
        scratch_shapes=[
            pltpu.VMEM((2, 2048, 512), bf),
            pltpu.VMEM((2, 2048, 128), bf),
            pltpu.VMEM((2, 2048, 512), bf),
            pltpu.VMEM((2, 128, 2048), bf),
            pltpu.VMEM((256, 128), bf),
            pltpu.VMEM((2, 512, 896), bf),
            pltpu.VMEM((512, 128), jnp.float32),
            pltpu.VMEM((512, 128), jnp.float32),
            pltpu.VMEM((512, 512), jnp.float32),
            pltpu.VMEM((64, 32, 512), jnp.float32),
            pltpu.VMEM((64, 64, 512), bf),
            pltpu.SemaphoreType.DMA((copies,)), pltpu.SemaphoreType.DMA((copies,)),
            pltpu.SemaphoreType.DMA((6,)), pltpu.SemaphoreType.DMA((10,)),
        ],
        compiler_params=pltpu.CompilerParams(collective_id=0, has_side_effects=True, vmem_limit_bytes=58 * 2**20),
        cost_estimate=pl.CostEstimate(flops=18 * 10**9, bytes_accessed=40 * 2**20, transcendentals=8 * 2**20),
    )(cache_len, live_rows, queries, ropes, lat_cache, rope_cache, new_lat, new_rope, ancestors, value_up, out_proj)


def project_kernel(
    ctx_hbm, up_hbm, blk_hbm, out_hbm,
    ctx, up, blk, hv, act, part, relay, sums, near, fin, got, send, recv, local,
):
    m = Mover(send, recv)
    x, y = m.x, m.y
    loads = {}
    def load(name, src, dst):
        copy = pltpu.make_async_copy(src, dst, local.at[len(loads)])
        copy.start()
        loads[name] = copy
    load("ctx", ctx_hbm, ctx)
    for dx in (0, 1, 3, 2):
        kb = nbr(x, dx)
        load(dx, up_hbm.at[kb], up.at[dx])
    load("blk", blk_hbm, blk)
    m.greet([dict(x=1), dict(x=-1), dict(x=2), dict(y=1), dict(y=-1), dict(y=2)])

    sent = []

    def go(src, dst, **step):
        copy = m.go(src, dst, **step)
        sent.append(copy)
        return copy

    def values(dx, target):
        kb = nbr(x, dx)
        loads[dx].wait()

        def heads(i, carry):
            h = kb * 16 + i
            v = jnp.dot(ctx[h], up[dx, i], preferred_element_type=jnp.float32)
            target[:, pl.ds(pl.multiple_of(i * 128, 128), 128)] = v.astype(jnp.bfloat16)
            return carry

        lax.fori_loop(0, 16, heads, 0, unroll=4)

    loads["ctx"].wait()
    came = {}
    values(0, act.at[0, 0])
    ys = {(0, 1): go(act.at[0, 0], act.at[3, 0], y=1), (0, 3): go(act.at[0, 0], act.at[1, 0], y=-1)}
    for dx in (1, 3, 2):
        values(dx, hv.at[dx])
        came[-dx % 4] = go(hv.at[dx], act.at[0, -dx % 4], x=dx)
    loads["blk"].wait()

    def product(yr, xr):
        def columns(h, carry):
            part[yr, xr, h] = jnp.dot(act[yr, xr], blk[h], preferred_element_type=jnp.float32).astype(jnp.bfloat16)
            return carry

        lax.fori_loop(0, 2, columns, 0)

    def spread(xr):
        ys[(xr, 1)] = go(act.at[0, xr], act.at[3, xr], y=1)
        ys[(xr, 3)] = go(act.at[0, xr], act.at[1, xr], y=-1)

    far, direct, summed = {}, {}, {}

    def send_far(yr):
        far[(yr, 0)] = go(part.at[yr, 2, 0], relay.at[yr, 0], x=1)
        far[(yr, 1)] = go(part.at[yr, 2, 1], relay.at[yr, 1], x=-1)

    def send_direct(yr, xr):
        if xr == 1:
            direct[(yr, 1)] = go(part.at[yr, 1, 1], near.at[yr, 0, 1], x=1)
        else:
            direct[(yr, 3)] = go(part.at[yr, 3, 0], near.at[yr, 1, 0], x=-1)

    def add(a, b):
        return a.astype(jnp.float32) + b.astype(jnp.float32)

    def send_sum(yr, side):
        far[(yr, side)].wait_recv()
        xr = 1 if side == 0 else 3
        sums[yr, side] = add(part[yr, xr, side], relay[yr, side]).astype(jnp.bfloat16)
        summed[(yr, side)] = go(sums.at[yr, side], near.at[yr, side, side], x=1 if side == 0 else -1)

    out_copies = []

    def write(yr):
        cb = nbr(y, yr)
        for h in range(2):
            cols = pl.ds(pl.multiple_of(cb * 1792 + h * 896, 128), 896)
            copy = pltpu.make_async_copy(got.at[yr, h], out_hbm.at[:, cols], local.at[6 + yr * 2 + h])
            copy.start()
            out_copies.append(copy)

    home = {}

    def finish(yr):
        direct[(yr, 1)].wait_recv()
        direct[(yr, 3)].wait_recv()
        summed[(yr, 0)].wait_recv()
        summed[(yr, 1)].wait_recv()
        for h in range(2):
            total = (add(part[yr, 0, h], near[yr, 0, h]) + near[yr, 1, h].astype(jnp.float32)).astype(jnp.bfloat16)
            if yr:
                fin[yr, h] = total
            else:
                got[0, h] = total
        if yr:
            home[-yr % 4] = go(fin.at[yr], got.at[-yr % 4], y=yr)
        else:
            write(0)

    def arrived(yr, xr):
        if yr == 3:
            ys[(xr, 1)].wait_recv()
        elif yr == 1:
            ys[(xr, 3)].wait_recv()
        else:
            ys[(xr, 2)].wait_recv()

    def forward(xr):
        if xr < 2:
            ys[(xr, 2)] = go(act.at[3, xr], act.at[2, xr], y=1)
        else:
            ys[(xr, 2)] = go(act.at[1, xr], act.at[2, xr], y=-1)

    product(0, 0)
    came[1].wait_recv()
    spread(1)
    product(0, 1)
    came[3].wait_recv()
    product(0, 3)
    for yr in (3, 1):
        arrived(yr, 0)
        product(yr, 0)
    came[2].wait_recv()
    spread(2)
    spread(3)
    product(0, 2)
    send_far(0)
    send_direct(0, 1)
    send_direct(0, 3)
    for yr in (3, 1):
        arrived(yr, 1)
        product(yr, 1)
    send_sum(0, 0)
    send_sum(0, 1)
    send_direct(3, 1)
    send_direct(1, 1)
    arrived(1, 2)
    forward(2)
    forward(0)
    product(1, 2)
    send_far(1)
    arrived(3, 2)
    product(3, 2)
    send_far(3)
    finish(0)
    arrived(1, 3)
    forward(3)
    forward(1)
    product(1, 3)
    send_direct(1, 3)
    arrived(3, 3)
    product(3, 3)
    send_direct(3, 3)
    for yr in (1, 3):
        send_sum(yr, 0)
        send_sum(yr, 1)
    arrived(2, 2)
    product(2, 2)
    send_far(2)
    arrived(2, 0)
    product(2, 0)
    finish(1)
    finish(3)
    arrived(2, 3)
    product(2, 3)
    send_direct(2, 3)
    arrived(2, 1)
    product(2, 1)
    send_direct(2, 1)
    send_sum(2, 0)
    send_sum(2, 1)
    finish(2)
    for yr in (1, 3, 2):
        home[yr].wait_recv()
        write(yr)
    for copy in sent:
        copy.wait_send()
    for copy in out_copies:
        copy.wait()


def project(context, all_up, block):
    bf = jnp.bfloat16
    copies = 48
    return pl.pallas_call(
        project_kernel,
        out_shape=jax.ShapeDtypeStruct((64, 7168), bf),
        in_specs=[pl.BlockSpec(memory_space=pl.ANY)] * 3,
        out_specs=pl.BlockSpec(memory_space=pl.ANY),
        scratch_shapes=[
            pltpu.VMEM((64, 64, 512), bf),
            pltpu.VMEM((4, 16, 512, 128), bf),
            pltpu.VMEM((2, 2048, 896), bf),
            pltpu.VMEM((4, 64, 2048), bf),
            pltpu.VMEM((4, 4, 64, 2048), bf),
            pltpu.VMEM((4, 4, 2, 64, 896), bf),
            pltpu.VMEM((4, 2, 64, 896), bf),
            pltpu.VMEM((4, 2, 64, 896), bf),
            pltpu.VMEM((4, 2, 2, 64, 896), bf),
            pltpu.VMEM((4, 2, 64, 896), bf),
            pltpu.VMEM((4, 2, 64, 896), bf),
            pltpu.SemaphoreType.DMA((copies,)), pltpu.SemaphoreType.DMA((copies,)), pltpu.SemaphoreType.DMA((14,)),
        ],
        compiler_params=pltpu.CompilerParams(collective_id=1, has_side_effects=True, vmem_limit_bytes=56 * 2**20),
        cost_estimate=pl.CostEstimate(flops=8 * 10**9, bytes_accessed=24 * 2**20, transcendentals=0),
    )(context, all_up.reshape(4, 16, 512, 128), block.reshape(2, 2048, 896))


def per_device(query_lat, query_rope, lat_cache, rope_cache, new_lat, new_rope, cache_len, live_rows, ancestors,
               value_up, out_proj):
    context, all_up, block = attend(
        query_lat, query_rope, lat_cache, rope_cache, new_lat, new_rope, cache_len, live_rows, ancestors,
        value_up, out_proj)
    return project(context, all_up, block)


def solution(mesh):
    both = ("grp", "dp")
    in_specs = (
        P(both, None, None, None), P(both, None, None), P(both, None, None), P(both, None, None),
        P(both, None, None), P(both, None, None), P(both), P(both), P(both, None, None),
        P("dp", None, None), P("dp", None),
    )
    return jax.shard_map(per_device, mesh=mesh, in_specs=in_specs, out_specs=P(both, None), check_vma=False)
```

```python
import functools
import jax
import jax.numpy as jnp
from jax import lax
from jax.experimental import pallas as pl
from jax.experimental.pallas import tpu as pltpu
from jax.sharding import PartitionSpec as P

score_scale = 192.0 ** (-0.5)
log2_e = 1.4426950408889634
very_negative = -1e30
MESH = pl.DeviceIdType.MESH
nt = (((1,), (1,)), ((), ()))


def nbr(base, step):
    return lax.rem(base + step % 4, 4) if step % 4 else base


class Remote:
    def __init__(self, mover, src, dst, step):
        self.mover, self.src, self.dst, self.step = mover, src, dst, step
        self.number = mover.used
        mover.used += 1
        mover.made.append(self)

    def copy(self):
        m = self.mover
        return pltpu.make_async_remote_copy(
            src_ref=self.src(), dst_ref=self.dst(), send_sem=m.send.at[self.number], recv_sem=m.recv.at[self.number],
            device_id=m.device(**self.step), device_id_type=MESH)

    def start(self):
        self.copy().start()
        return self

    def wait_recv(self):
        self.copy().wait_recv()

    def wait_send(self):
        self.copy().wait_send()


class Mover:
    def __init__(self, send, recv):
        self.send, self.recv, self.used, self.made = send, recv, 0, []
        grp, dp = lax.axis_index("grp"), lax.axis_index("dp")
        self.y, self.c = grp // 2, lax.rem(grp, 2)
        self.x, self.z = dp // 4, lax.rem(dp, 4)

    def device(self, x=0, y=0, z=0, c=0):
        cc = lax.rem(self.c + c, 2) if c else self.c
        return (nbr(self.y, y) * 2 + cc, nbr(self.x, x) * 4 + nbr(self.z, z))

    def greet(self, steps):
        barrier = pltpu.get_barrier_semaphore()
        for step in steps:
            pl.semaphore_signal(barrier, inc=1, device_id=self.device(**step), device_id_type=MESH)
        pl.semaphore_wait(barrier, len(steps))

    def later(self, src, dst, **step):
        return Remote(self, src, dst, step)

    def go(self, src, dst, **step):
        return Remote(self, lambda: src, lambda: dst, step).start()


def gather_plan(m, up_ref, proj_ref, all_ref, blk_ref, local):
    x, y, z, c = m.x, m.y, m.z, m.c
    shard = x * 4 + z
    half = pl.ds(pl.multiple_of(c * 256, 256), 256)
    pq = [pl.ds(pl.multiple_of(c * 256 + i * 128, 128), 128) for i in range(2)]
    column = lambda base: pl.ds(base * 4, 4)
    lower = lambda base: pl.ds(base * 4, 2)
    upper = lambda base: pl.ds(base * 4 + 2, 2)
    xl, xr, xo = nbr(x, -1), nbr(x, 1), nbr(x, 2)
    yl, yr, yo = nbr(y, -1), nbr(y, 1), nbr(y, 2)
    zl, zr, zo = nbr(z, -1), nbr(z, 1), nbr(z, 2)

    def at(ref, *index):
        return lambda: ref.at[index]

    def same(ref, *index, **step):
        view = at(ref, *index)
        return m.later(view, view, **step)

    def cols(h):
        return pl.ds(pl.multiple_of(y * 1792 + h * 896, 128), 896)

    own = [lambda: pltpu.make_async_copy(up_ref.at[y, half], all_ref.at[shard, y, half], local.at[0])]
    for h in range(2):
        own.append(lambda h=h: pltpu.make_async_copy(proj_ref.at[:, cols(h)], blk_ref.at[h, z], local.at[1 + h]))

    twins = {}

    def twin(name, ref, *index):
        twins.setdefault(name, []).append(same(ref, *index, c=1))

    zs = [m.later(at(up_ref, y, half), at(all_ref, shard, y, half), z=s) for s in (1, -1, 2)]
    mine = at(proj_ref, slice(None), pl.ds(pl.multiple_of(y * 1792 + c * 896, 128), 896))
    w = [m.later(mine, at(blk_ref, c, z), z=s) for s in (1, -1)]
    wf = [same(blk_ref, c, zl, pl.ds(0, 256), z=1), same(blk_ref, c, zr, pl.ds(256, 256), z=-1)]
    xp = [same(all_ref, column(x), y, pq[0], x=s) for s in (1, -1)]
    yq = [same(all_ref, column(x), y, pq[1], y=s) for s in (1, -1)]
    xpf = [same(all_ref, lower(xl), y, pq[0], x=1), same(all_ref, upper(xr), y, pq[0], x=-1)]
    yqf = [same(all_ref, lower(x), yl, pq[1], y=1), same(all_ref, upper(x), yr, pq[1], y=-1)]
    bases_x, bases_y = (x, xl, xr, xo), (y, yl, yr, yo)
    yp = [[same(all_ref, column(b), y, pq[0], y=s) for s in (1, -1)] for b in bases_x]
    xq = [[same(all_ref, column(x), b, pq[1], x=s) for s in (1, -1)] for b in bases_y]
    ypf = [[same(all_ref, lower(b), yl, pq[0], y=1), same(all_ref, upper(b), yr, pq[0], y=-1)] for b in bases_x]
    xqf = [[same(all_ref, lower(xl), b, pq[1], x=1), same(all_ref, upper(xr), b, pq[1], x=-1)] for b in bases_y]

    twin("spread", all_ref, column(x), y, half)
    for b in (xl, xr):
        twin("near", all_ref, column(b), y, pq[0])
    for b in (yl, yr):
        twin("near", all_ref, column(x), b, pq[1])
    twin("far", all_ref, column(xo), y, pq[0])
    twin("far", all_ref, column(x), yo, pq[1])
    for k in range(4):
        name = "pass%d" % min(k + 1, 3)
        for b in (yl, yr):
            twin(name, all_ref, column(bases_x[k]), b, pq[0])
        for b in (xl, xr):
            twin(name, all_ref, column(b), bases_y[k], pq[1])
        name = "tail%d" % (k // 2)
        twin(name, all_ref, column(bases_x[k]), yo, pq[0])
        twin(name, all_ref, column(xo), bases_y[k], pq[1])
    twin("weights", blk_ref, c, zl)
    twin("weights", blk_ref, c, zr)
    twin("last", blk_ref, c, zo)

    def start(*copies):
        for copy in copies:
            copy.start()

    def got(*copies):
        for copy in copies:
            copy.wait_recv()

    def first():
        for load in own:
            load().start()
        m.greet([dict(x=1), dict(x=-1), dict(x=2), dict(y=1), dict(y=-1), dict(y=2),
                 dict(z=1), dict(z=-1), dict(z=2), dict(c=1)])
        start(*zs)

    def spread():
        own[0]().wait()
        got(*zs)
        start(*w)
        start(*xp, *yq, *yp[0], *xq[0])
        start(*twins["spread"])

    def near():
        got(*xp)
        start(*xpf)
        got(*yq)
        start(*yqf)
        start(*yp[1], *xq[1], *yp[2], *xq[2])
        start(*twins["near"])

    def far():
        got(*xpf, *yqf)
        got(*yp[0], *xq[0])
        start(*ypf[0], *xqf[0], *yp[3], *xq[3])
        start(*twins["far"])

    def pass_on(k):
        def step():
            got(*yp[k], *xq[k])
            start(*ypf[k], *xqf[k])
            start(*twins["pass%d" % k])
        return step

    def weights():
        got(*w)
        start(*wf)
        start(*twins["weights"])

    def tail(name, ks):
        def step():
            for k in ks:
                got(*ypf[k], *xqf[k])
            start(*twins[name])
        return step

    def ready():
        for name, group in twins.items():
            if name not in ("weights", "last"):
                got(*group)

    def block_ready():
        got(*wf)
        start(*twins["last"])
        got(*twins["weights"], *twins["last"])
        for load in own[1:]:
            load().wait()

    return dict(first=first, spread=spread, near=near, far=far, pass1=pass_on(1), pass2=pass_on(2), pass3=pass_on(3),
                weights=weights, ready=ready, block_ready=block_ready, tail0=tail("tail0", (0, 1)), tail1=tail("tail1", (2, 3)))


schedule = {
    0: ["spread"], 2: ["near"], 4: ["far"], 5: ["pass1"], 6: ["pass2"], 7: ["pass3"], 8: ["tail0"], 9: ["tail1"],
    11: ["open", "weights"], 13: ["side"], 14: ["across"],
}


def lane_sum(w):
    parts = [w[:, c * 128:(c + 1) * 128] for c in range(w.shape[1] // 128)]
    while len(parts) > 1:
        parts = [a + b for a, b in zip(parts[::2], parts[1::2])] + (parts[-1:] if len(parts) % 2 else [])
    return parts[0]


def add(a, b):
    return a.astype(jnp.float32) + b.astype(jnp.float32)


class Project:
    def __init__(self, m, out_hbm, ctx, up, blk, hv, act, part, relay, sums, near, fin, got, writes):
        self.m, self.out_hbm, self.ctx, self.up, self.blk, self.hv, self.act, self.part = (
            m, out_hbm, ctx, up, blk, hv, act, part)
        self.relay, self.sums, self.near, self.fin, self.got, self.writes = relay, sums, near, fin, got, writes

        def copy(src, i, dst, j, **step):
            return m.later(lambda: src.at[i], lambda: dst.at[j], **step)

        both, four = range(2), range(4)
        self.swap = {(q, dx): copy(hv, (q, dx), act, (q, 0, -dx % 4), x=dx) for q in both for dx in (1, 3, 2)}
        self.wide = {(q, xr, s): copy(act, (q, 0, xr), act, (q, -s % 4, xr), y=s)
                     for q in both for xr in four for s in (1, -1)}
        self.on = {(q, xr): (copy(act, (q, 3, xr), act, (q, 2, xr), y=1) if xr < 2 else
                             copy(act, (q, 1, xr), act, (q, 2, xr), y=-1)) for q in both for xr in four}
        self.far, self.direct, self.summed, self.home = {}, {}, {}, {}
        for q in both:
            for yr in four:
                for side, xr, way in ((0, 1, 1), (1, 3, -1)):
                    k = (q, yr, side)
                    self.far[k] = copy(part, (q, yr, 2, side), relay, (q, yr, side), x=way)
                    self.direct[k] = copy(part, (q, yr, xr, 1 - side), near, (q, yr, side, 1 - side), x=way)
                    self.summed[k] = copy(sums, (q, yr, side), near, (q, yr, side, side), x=way)
                if yr:
                    self.home[q, yr] = copy(fin, (q, yr), got, (q, -yr % 4), y=yr)

    def values(self, q, dx, target):
        kb = nbr(self.m.x, dx)

        def heads(i, carry):
            h = kb * 16 + i
            v = jnp.dot(self.ctx[h], self.up[h // 4, lax.rem(h, 4)], preferred_element_type=jnp.float32)
            target[:, pl.ds(pl.multiple_of(i * 128, 128), 128)] = v.astype(jnp.bfloat16)
            return carry

        lax.fori_loop(0, 16, heads, 0, unroll=4)

    def open(self, q):
        for dx in (1, 3, 2):
            self.values(q, dx, self.hv.at[q, dx])
            self.swap[q, dx].start()
        self.values(q, 0, self.act.at[q, 0, 0])

    def widen(self, q, xr):
        if xr:
            self.swap[q, -xr % 4].wait_recv()
        self.wide[q, xr, 1].start()
        self.wide[q, xr, -1].start()

    def arrived(self, q, yr, xr):
        if yr == 2:
            self.on[q, xr].wait_recv()
        else:
            self.wide[q, xr, 1 if yr == 3 else -1].wait_recv()

    def pass_on(self, q, *xrs):
        for xr in xrs:
            self.arrived(q, 3 if xr < 2 else 1, xr)
            self.on[q, xr].start()

    def rest(self, q):
        for xr in (2, 3):
            self.arrived(q, 3, xr)
        for xr in (0, 1):
            self.arrived(q, 1, xr)

    def product(self, q, yr):
        def columns(h, carry):
            rows = self.act[q, yr].reshape(128, 2048)
            p = jnp.dot(rows, self.blk[h].reshape(2048, 896), preferred_element_type=jnp.float32).astype(jnp.bfloat16)
            for xr in range(4):
                self.part[q, yr, xr, h] = p[xr * 32:(xr + 1) * 32]
            return carry

        lax.fori_loop(0, 2, columns, 0)
        for side in range(2):
            self.far[q, yr, side].start()
        for side in range(2):
            self.direct[q, yr, side].start()

    def pass_sums(self, q, yr):
        for side, xr in ((0, 1), (1, 3)):
            self.far[q, yr, side].wait_recv()
            self.sums[q, yr, side] = add(self.part[q, yr, xr, side], self.relay[q, yr, side]).astype(jnp.bfloat16)
            self.summed[q, yr, side].start()

    def write(self, q, yr):
        cb = nbr(self.m.y, yr)
        copies = []
        for h in range(2):
            cols = pl.ds(pl.multiple_of(cb * 1792 + h * 896, 128), 896)
            copies.append(pltpu.make_async_copy(
                self.got.at[q, yr, h], self.out_hbm.at[pl.ds(q * 32, 32), cols], self.writes.at[q * 8 + yr * 2 + h]))
        return copies

    def finish(self, q, yr):
        for side in range(2):
            self.direct[q, yr, side].wait_recv()
            self.summed[q, yr, side].wait_recv()
        for h in range(2):
            total = (add(self.part[q, yr, 0, h], self.near[q, yr, 0, h])
                     + self.near[q, yr, 1, h].astype(jnp.float32)).astype(jnp.bfloat16)
            if yr:
                self.fin[q, yr, h] = total
            else:
                self.got[q, 0, h] = total
        if yr:
            self.home[q, yr].start()
        else:
            for copy in self.write(q, 0):
                copy.start()


def layer_kernel(
    len_ref, live_ref, q_hbm, qr_hbm, lat_hbm, rope_hbm, new_ref, newr_ref, anc_ref, up_ref, proj_ref,
    out_hbm,
    q_ref, raw_s, qr_ref, lat_ref, rope_ref, top_s, tot_s, acc_s, turn_s, ctx_s, all_ref, blk_ref,
    hv, act, part, relay, sums, near, fin, got,
    send, recv, local, loads, writes,
):
    factor = score_scale * log2_e
    heads, width, key_blk, sub = 64, 512, 1024, 256
    m = Mover(send, recv)
    plan = gather_plan(m, up_ref, proj_ref, all_ref, blk_ref, local)
    project = Project(m, out_hbm, ctx_s, all_ref, blk_ref, hv, act, part, relay, sums, near, fin, got, writes)

    def begin():
        plan["ready"]()
        project.open(0)
        project.widen(0, 0)

    def side():
        project.widen(0, 1)
        project.widen(0, 3)

    plan.update(open=begin, side=side, across=lambda: project.widen(0, 2))

    def fetch_ropes(r):
        return pltpu.make_async_copy(qr_hbm.at[r], raw_s.at[r], loads.at[6 + r])

    def arrange_ropes(r):
        fetch_ropes(r).wait()
        lane = lax.broadcasted_iota(jnp.int32, (32, 128), 1)
        after = jnp.where(lane == 64, 1.0, 0.0)

        def pair(i, carry):
            both = raw_s[r, :, pl.ds(pl.multiple_of(i * 128, 128), 128)].astype(jnp.float32)
            turn_s[2 * i, :, pl.ds(0, 128)] = jnp.where(lane < 64, both, after)
            turn_s[2 * i + 1, :, pl.ds(0, 128)] = jnp.where(lane < 64, pltpu.roll(both, 64, 1), after)
            return carry

        lax.fori_loop(0, heads // 2, pair, 0, unroll=4)
        for block in range(4):
            turned = jnp.swapaxes(turn_s[:, pl.ds(block * 8, 8), pl.ds(0, 128)], 0, 1)
            qr_ref[r, pl.ds(block * 512, 512), :] = turned.reshape(512, 128).astype(jnp.bfloat16)

    def fetch(r):
        pairs = ((q_hbm.at[r], q_ref.at[r]), (lat_hbm.at[r], lat_ref.at[r]),
                 (rope_hbm.at[r], rope_ref.at[r, pl.ds(0, 64)]))
        return [pltpu.make_async_copy(src, dst, loads.at[r * 3 + i]) for i, (src, dst) in enumerate(pairs)]

    for r in range(2):
        for copy in fetch(r):
            copy.start()
        fetch_ropes(r).start()
    plan["first"]()
    for r in range(2):
        position = lax.broadcasted_iota(jnp.int32, (64, 2048), 1)
        row = lax.broadcasted_iota(jnp.int32, (64, 2048), 0)
        outside = jnp.logical_and(row == 0, position >= len_ref[r])
        arrange_ropes(r)
        rope_ref[r, pl.ds(64, 64), :] = jnp.where(outside, very_negative, 0.0).astype(jnp.bfloat16)

    def step(i, carry):
        for r in range(2):
            @pl.when(i == r * 8)
            def _():
                for copy in fetch(r):
                    copy.wait()

        request = i // 8
        block = lax.rem(i, 8) // 2
        key = lax.rem(i, 2)
        row0 = block * 8

        def queries(part):
            start = pl.multiple_of(row0 * heads + part * sub, sub)
            return q_ref[request, pl.ds(start, sub), :], qr_ref[request, pl.ds(start, sub), :]

        @pl.when(key == 0)
        def _():
            for part in range(2):
                q, qr = queries(part)
                rows = pl.ds(part * sub, sub)
                s = lax.dot_general(q, new_ref[request], nt, preferred_element_type=jnp.float32)
                s = s + lax.dot_general(qr[:, :64], newr_ref[request], nt, preferred_element_type=jnp.float32)
                s = s * factor
                anc = anc_ref[request, pl.ds(row0 + part * 4, 4), :]
                bias = jnp.where(anc > 0, 0.0, very_negative)
                s = (s.reshape(4, heads, 32) + bias[:, None, :]).reshape(sub, 32)
                top = jnp.max(s, axis=1, keepdims=True)
                w = jnp.exp2(s - top)
                top_s[rows, :] = jnp.broadcast_to(top, (sub, 128))
                tot_s[rows, :] = jnp.where(lax.broadcasted_iota(jnp.int32, (sub, 128), 1) == 0,
                                           jnp.sum(w, axis=1, keepdims=True), 0.0)
                acc_s[rows, :] = jnp.dot(w.astype(jnp.bfloat16), new_ref[request], preferred_element_type=jnp.float32)

        offset = pl.multiple_of(key * key_blk, key_blk)
        keys = lat_ref[request, pl.ds(offset, key_blk), :]
        rope_keys = rope_ref[request, :, pl.ds(offset, key_blk)]
        scores = []
        for part in range(2):
            q, qr = queries(part)
            scores.append(lax.dot_general(q, keys, nt, preferred_element_type=jnp.float32)
                          + jnp.dot(qr, rope_keys, preferred_element_type=jnp.float32))
        for part in range(2):
            s = scores[part]
            rows = pl.ds(part * sub, sub)
            old = top_s[rows, :]
            new = jnp.maximum(old, jnp.max(s, axis=1, keepdims=True) * factor)
            rescale = jnp.exp2(old - new)
            w = jnp.exp2(s * factor - new[:, :1])
            tot_s[rows, :] = tot_s[rows, :] * rescale + lane_sum(w)
            top_s[rows, :] = new
            acc_s[rows, :] = acc_s[rows, :] * rescale[:, :1] + jnp.dot(
                w.astype(jnp.bfloat16), keys, preferred_element_type=jnp.float32)

        @pl.when(key == 1)
        def _():
            total = jnp.sum(tot_s[...], axis=1, keepdims=True)
            ctx = (acc_s[...] * (1.0 / total)).reshape(8, heads, width)
            alive = row0 + lax.broadcasted_iota(jnp.int32, (8, heads, 1), 0) < live_ref[request]
            ctx = jnp.where(alive, ctx, 0.0)
            turn_s[:, pl.ds(pl.multiple_of(row0, 8), 8), :] = jnp.swapaxes(ctx, 0, 1)

        @pl.when(i == 7)
        def _():
            ctx_s[...] = turn_s[...].astype(jnp.bfloat16)

        for point, names in schedule.items():
            @pl.when(i == point)
            def _():
                for name in names:
                    plan[name]()
        return carry

    lax.fori_loop(0, 16, step, 0)
    ctx_s[...] = turn_s[...].astype(jnp.bfloat16)
    p = project
    p.open(1)
    plan["block_ready"]()
    p.product(0, 0)
    p.pass_on(0, 0, 2)
    p.widen(1, 0)
    p.pass_sums(0, 0)
    p.pass_on(0, 1, 3)
    p.rest(0)
    p.product(0, 3)
    p.product(0, 1)
    p.widen(1, 1)
    p.widen(1, 3)
    p.pass_sums(0, 3)
    p.pass_sums(0, 1)
    p.widen(1, 2)
    p.finish(0, 0)
    for xr in range(4):
        p.arrived(0, 2, xr)
    p.product(0, 2)
    p.product(1, 0)
    p.finish(0, 3)
    p.finish(0, 1)
    p.pass_on(1, 0, 2)
    p.pass_sums(0, 2)
    p.pass_sums(1, 0)
    p.pass_on(1, 1, 3)
    p.rest(1)
    p.product(1, 3)
    p.product(1, 1)
    p.finish(0, 2)
    p.pass_sums(1, 3)
    p.pass_sums(1, 1)
    p.finish(1, 0)
    for xr in range(4):
        p.arrived(1, 2, xr)
    p.product(1, 2)
    p.finish(1, 3)
    p.finish(1, 1)
    p.pass_sums(1, 2)
    p.finish(1, 2)
    for q in range(2):
        for yr in (1, 3, 2):
            p.home[q, -yr % 4].wait_recv()
            for copy in p.write(q, yr):
                copy.start()
    for copy in m.made:
        copy.wait_send()
    for q in range(2):
        for yr in range(4):
            for copy in p.write(q, yr):
                copy.wait()


def layer(query_lat, query_rope, lat_cache, rope_cache, new_lat, new_rope, cache_len, live_rows, ancestors,
           value_up, out_proj):
    bf = jnp.bfloat16
    queries = query_lat.reshape(2, 2048, 512)
    anywhere = pl.BlockSpec(memory_space=pl.ANY)
    smem, vmem = pl.BlockSpec(memory_space=pltpu.SMEM), pl.BlockSpec(memory_space=pltpu.VMEM)
    copies = 176
    return pl.pallas_call(
        layer_kernel,
        out_shape=jax.ShapeDtypeStruct((64, 7168), bf),
        in_specs=[smem, smem] + [anywhere] * 4 + [vmem] * 3 + [anywhere] * 2,
        out_specs=anywhere,
        scratch_shapes=[
            pltpu.VMEM((2, 2048, 512), bf),
            pltpu.VMEM((2, 32, 4096), bf),
            pltpu.VMEM((2, 2048, 128), bf),
            pltpu.VMEM((2, 2048, 512), bf),
            pltpu.VMEM((2, 128, 2048), bf),
            pltpu.VMEM((512, 128), jnp.float32),
            pltpu.VMEM((512, 128), jnp.float32),
            pltpu.VMEM((512, 512), jnp.float32),
            pltpu.VMEM((64, 32, 512), jnp.float32),
            pltpu.VMEM((64, 32, 512), bf),
            pltpu.VMEM((16, 4, 512, 128), bf),
            pltpu.VMEM((2, 4, 512, 896), bf),
            pltpu.VMEM((2, 4, 32, 2048), bf),
            pltpu.VMEM((2, 4, 4, 32, 2048), bf),
            pltpu.VMEM((2, 4, 4, 2, 32, 896), bf),
            pltpu.VMEM((2, 4, 2, 32, 896), bf),
            pltpu.VMEM((2, 4, 2, 32, 896), bf),
            pltpu.VMEM((2, 4, 2, 2, 32, 896), bf),
            pltpu.VMEM((2, 4, 2, 32, 896), bf),
            pltpu.VMEM((2, 4, 2, 32, 896), bf),
            pltpu.SemaphoreType.DMA((copies,)), pltpu.SemaphoreType.DMA((copies,)),
            pltpu.SemaphoreType.DMA((3,)), pltpu.SemaphoreType.DMA((8,)), pltpu.SemaphoreType.DMA((16,)),
        ],
        compiler_params=pltpu.CompilerParams(collective_id=0, has_side_effects=True, vmem_limit_bytes=62 * 2**20),
        cost_estimate=pl.CostEstimate(flops=26 * 10**9, bytes_accessed=40 * 2**20, transcendentals=8 * 2**20),
    )(cache_len, live_rows, queries, query_rope, lat_cache, rope_cache, new_lat, new_rope, ancestors, value_up, out_proj)


def per_device(query_lat, query_rope, lat_cache, rope_cache, new_lat, new_rope, cache_len, live_rows, ancestors,
               value_up, out_proj):
    return layer(query_lat, query_rope, lat_cache, rope_cache, new_lat, new_rope, cache_len, live_rows, ancestors,
                 value_up, out_proj)


def solution(mesh):
    both = ("grp", "dp")
    in_specs = (
        P(both, None, None, None), P(both, None, None), P(both, None, None), P(both, None, None),
        P(both, None, None), P(both, None, None), P(both), P(both), P(both, None, None),
        P("dp", None, None), P("dp", None),
    )
    return jax.shard_map(per_device, mesh=mesh, in_specs=in_specs, out_specs=P(both, None), check_vma=False)
```

```python
import functools
import jax
import jax.numpy as jnp
from jax import lax
from jax.experimental import pallas as pl
from jax.experimental.pallas import tpu as pltpu
from jax.sharding import PartitionSpec as P

score_scale = 192.0 ** (-0.5)
log2_e = 1.4426950408889634
very_negative = -1e30
MESH = pl.DeviceIdType.MESH
nt = (((1,), (1,)), ((), ()))


def nbr(base, step):
    return lax.rem(base + step % 4, 4) if step % 4 else base


class Remote:
    def __init__(self, mover, src, dst, step):
        self.mover, self.src, self.dst, self.step = mover, src, dst, step
        self.number = mover.used
        mover.used += 1
        mover.made.append(self)

    def copy(self):
        m = self.mover
        return pltpu.make_async_remote_copy(
            src_ref=self.src(), dst_ref=self.dst(), send_sem=m.send.at[self.number], recv_sem=m.recv.at[self.number],
            device_id=m.device(**self.step), device_id_type=MESH)

    def start(self):
        self.copy().start()
        return self

    def wait_recv(self):
        self.copy().wait_recv()

    def wait_send(self):
        self.copy().wait_send()


class Mover:
    def __init__(self, send, recv):
        self.send, self.recv, self.used, self.made = send, recv, 0, []
        grp, dp = lax.axis_index("grp"), lax.axis_index("dp")
        self.y, self.c = grp // 2, lax.rem(grp, 2)
        self.x, self.z = dp // 4, lax.rem(dp, 4)

    def device(self, x=0, y=0, z=0, c=0):
        cc = lax.rem(self.c + c, 2) if c else self.c
        return (nbr(self.y, y) * 2 + cc, nbr(self.x, x) * 4 + nbr(self.z, z))

    def greet(self, steps):
        barrier = pltpu.get_barrier_semaphore()
        for step in steps:
            pl.semaphore_signal(barrier, inc=1, device_id=self.device(**step), device_id_type=MESH)
        pl.semaphore_wait(barrier, len(steps))

    def later(self, src, dst, **step):
        return Remote(self, src, dst, step)

    def go(self, src, dst, **step):
        return Remote(self, lambda: src, lambda: dst, step).start()


def gather_plan(m, up_ref, proj_ref, all_ref, blk_ref, local):
    x, y, z, c = m.x, m.y, m.z, m.c
    shard = x * 4 + z
    half = pl.ds(pl.multiple_of(c * 256, 256), 256)
    pq = [pl.ds(pl.multiple_of(c * 256 + i * 128, 128), 128) for i in range(2)]
    column = lambda base: pl.ds(base * 4, 4)
    lower = lambda base: pl.ds(base * 4, 2)
    upper = lambda base: pl.ds(base * 4 + 2, 2)
    xl, xr, xo = nbr(x, -1), nbr(x, 1), nbr(x, 2)
    yl, yr, yo = nbr(y, -1), nbr(y, 1), nbr(y, 2)
    zl, zr, zo = nbr(z, -1), nbr(z, 1), nbr(z, 2)

    def at(ref, *index):
        return lambda: ref.at[index]

    def same(ref, *index, **step):
        view = at(ref, *index)
        return m.later(view, view, **step)

    def cols(h):
        return pl.ds(pl.multiple_of(y * 1792 + h * 896, 128), 896)

    own = [lambda: pltpu.make_async_copy(up_ref.at[y, half], all_ref.at[shard, y, half], local.at[0])]
    for h in range(2):
        own.append(lambda h=h: pltpu.make_async_copy(proj_ref.at[:, cols(h)], blk_ref.at[h, z], local.at[1 + h]))

    twins = {}

    def twin(name, ref, *index):
        twins.setdefault(name, []).append(same(ref, *index, c=1))

    zs = [m.later(at(up_ref, y, half), at(all_ref, shard, y, half), z=s) for s in (1, -1, 2)]
    mine = at(proj_ref, slice(None), pl.ds(pl.multiple_of(y * 1792 + c * 896, 128), 896))
    w = [m.later(mine, at(blk_ref, c, z), z=s) for s in (1, -1)]
    wf = [same(blk_ref, c, zl, pl.ds(0, 256), z=1), same(blk_ref, c, zr, pl.ds(256, 256), z=-1)]
    xp = [same(all_ref, column(x), y, pq[0], x=s) for s in (1, -1)]
    yq = [same(all_ref, column(x), y, pq[1], y=s) for s in (1, -1)]
    xpf = [same(all_ref, lower(xl), y, pq[0], x=1), same(all_ref, upper(xr), y, pq[0], x=-1)]
    yqf = [same(all_ref, lower(x), yl, pq[1], y=1), same(all_ref, upper(x), yr, pq[1], y=-1)]
    bases_x, bases_y = (x, xl, xr, xo), (y, yl, yr, yo)
    yp = [[same(all_ref, column(b), y, pq[0], y=s) for s in (1, -1)] for b in bases_x]
    xq = [[same(all_ref, column(x), b, pq[1], x=s) for s in (1, -1)] for b in bases_y]
    ypf = [[same(all_ref, lower(b), yl, pq[0], y=1), same(all_ref, upper(b), yr, pq[0], y=-1)] for b in bases_x]
    xqf = [[same(all_ref, lower(xl), b, pq[1], x=1), same(all_ref, upper(xr), b, pq[1], x=-1)] for b in bases_y]

    twin("spread", all_ref, column(x), y, half)
    for b in (xl, xr):
        twin("near", all_ref, column(b), y, pq[0])
    for b in (yl, yr):
        twin("near", all_ref, column(x), b, pq[1])
    twin("far", all_ref, column(xo), y, pq[0])
    twin("far", all_ref, column(x), yo, pq[1])
    for k in range(4):
        name = "pass%d" % min(k + 1, 3)
        for b in (yl, yr):
            twin(name, all_ref, column(bases_x[k]), b, pq[0])
        for b in (xl, xr):
            twin(name, all_ref, column(b), bases_y[k], pq[1])
        name = "tail%d" % (k // 2)
        twin(name, all_ref, column(bases_x[k]), yo, pq[0])
        twin(name, all_ref, column(xo), bases_y[k], pq[1])
    twin("weights", blk_ref, c, zl)
    twin("weights", blk_ref, c, zr)
    twin("last", blk_ref, c, zo)

    def start(*copies):
        for copy in copies:
            copy.start()

    def got(*copies):
        for copy in copies:
            copy.wait_recv()

    def first():
        for load in own:
            load().start()
        m.greet([dict(x=1), dict(x=-1), dict(x=2), dict(y=1), dict(y=-1), dict(y=2),
                 dict(z=1), dict(z=-1), dict(z=2), dict(c=1)])
        start(*zs)

    def spread():
        own[0]().wait()
        got(*zs)
        start(*w)
        start(*xp, *yq, *yp[0], *xq[0])
        start(*twins["spread"])

    def near():
        got(*xp)
        start(*xpf)
        got(*yq)
        start(*yqf)
        start(*yp[1], *xq[1], *yp[2], *xq[2])
        start(*twins["near"])

    def far():
        got(*xpf, *yqf)
        got(*yp[0], *xq[0])
        start(*ypf[0], *xqf[0], *yp[3], *xq[3])
        start(*twins["far"])

    def pass_on(k):
        def step():
            got(*yp[k], *xq[k])
            start(*ypf[k], *xqf[k])
            start(*twins["pass%d" % k])
        return step

    def weights():
        got(*w)
        start(*wf)
        start(*twins["weights"])

    def tail(name, ks):
        def step():
            for k in ks:
                got(*ypf[k], *xqf[k])
            start(*twins[name])
        return step

    def ready():
        for name, group in twins.items():
            if name not in ("weights", "last"):
                got(*group)

    def block_ready():
        got(*wf)
        start(*twins["last"])
        got(*twins["weights"], *twins["last"])
        for load in own[1:]:
            load().wait()

    return dict(first=first, spread=spread, near=near, far=far, pass1=pass_on(1), pass2=pass_on(2), pass3=pass_on(3),
                weights=weights, ready=ready, block_ready=block_ready, tail0=tail("tail0", (0, 1)), tail1=tail("tail1", (2, 3)))


schedule = {
    0: ["spread"], 1: ["near"], 2: ["far"], 3: ["pass1", "pass2"], 4: ["pass3", "tail0"], 5: ["tail1"],
    6: ["open", "weights"], 7: ["side", "across"],
}


def lane_sum(w):
    parts = [w[:, c * 128:(c + 1) * 128] for c in range(w.shape[1] // 128)]
    while len(parts) > 1:
        parts = [a + b for a, b in zip(parts[::2], parts[1::2])] + (parts[-1:] if len(parts) % 2 else [])
    return parts[0]


def add(a, b):
    return a.astype(jnp.float32) + b.astype(jnp.float32)


class Project:
    def __init__(self, m, out_hbm, ctx, up, blk, hv, act, part, relay, sums, near, fin, got, writes):
        self.m, self.out_hbm, self.ctx, self.up, self.blk, self.hv, self.act, self.part = (
            m, out_hbm, ctx, up, blk, hv, act, part)
        self.relay, self.sums, self.near, self.fin, self.got, self.writes = relay, sums, near, fin, got, writes

        def copy(src, i, dst, j, **step):
            return m.later(lambda: src.at[i], lambda: dst.at[j], **step)

        both, four = range(2), range(4)
        self.swap = {(q, dx): copy(hv, (q, dx), act, (q, 0, -dx % 4), x=dx) for q in both for dx in (1, 3, 2)}
        self.wide = {(q, xr, s): copy(act, (q, 0, xr), act, (q, -s % 4, xr), y=s)
                     for q in both for xr in four for s in (1, -1)}
        self.on = {(q, xr): (copy(act, (q, 3, xr), act, (q, 2, xr), y=1) if xr < 2 else
                             copy(act, (q, 1, xr), act, (q, 2, xr), y=-1)) for q in both for xr in four}
        self.far, self.direct, self.summed, self.home = {}, {}, {}, {}
        for q in both:
            for yr in four:
                for side, xr, way in ((0, 1, 1), (1, 3, -1)):
                    k = (q, yr, side)
                    self.far[k] = copy(part, (q, yr, 2, side), relay, (q, yr, side), x=way)
                    self.direct[k] = copy(part, (q, yr, xr, 1 - side), near, (q, yr, side, 1 - side), x=way)
                    self.summed[k] = copy(sums, (q, yr, side), near, (q, yr, side, side), x=way)
                if yr:
                    self.home[q, yr] = copy(fin, (q, yr), got, (q, -yr % 4), y=yr)

    def values(self, q, dx, target):
        kb = nbr(self.m.x, dx)

        def heads(i, carry):
            h = kb * 16 + i
            v = jnp.dot(self.ctx[h], self.up[h // 4, lax.rem(h, 4)], preferred_element_type=jnp.float32)
            target[:, pl.ds(pl.multiple_of(i * 128, 128), 128)] = v.astype(jnp.bfloat16)
            return carry

        lax.fori_loop(0, 16, heads, 0, unroll=4)

    def open(self, q):
        for dx in (1, 3, 2):
            self.values(q, dx, self.hv.at[q, dx])
            self.swap[q, dx].start()
        self.values(q, 0, self.act.at[q, 0, 0])

    def widen(self, q, xr):
        if xr:
            self.swap[q, -xr % 4].wait_recv()
        self.wide[q, xr, 1].start()
        self.wide[q, xr, -1].start()

    def arrived(self, q, yr, xr):
        if yr == 2:
            self.on[q, xr].wait_recv()
        else:
            self.wide[q, xr, 1 if yr == 3 else -1].wait_recv()

    def pass_on(self, q, *xrs):
        for xr in xrs:
            self.arrived(q, 3 if xr < 2 else 1, xr)
            self.on[q, xr].start()

    def rest(self, q):
        for xr in (2, 3):
            self.arrived(q, 3, xr)
        for xr in (0, 1):
            self.arrived(q, 1, xr)

    def product(self, q, yr):
        def columns(h, carry):
            rows = self.act[q, yr].reshape(128, 2048)
            p = jnp.dot(rows, self.blk[h].reshape(2048, 896), preferred_element_type=jnp.float32).astype(jnp.bfloat16)
            for xr in range(4):
                self.part[q, yr, xr, h] = p[xr * 32:(xr + 1) * 32]
            return carry

        lax.fori_loop(0, 2, columns, 0)
        for side in range(2):
            self.far[q, yr, side].start()
        for side in range(2):
            self.direct[q, yr, side].start()

    def pass_sums(self, q, yr):
        for side, xr in ((0, 1), (1, 3)):
            self.far[q, yr, side].wait_recv()
            self.sums[q, yr, side] = add(self.part[q, yr, xr, side], self.relay[q, yr, side]).astype(jnp.bfloat16)
            self.summed[q, yr, side].start()

    def write(self, q, yr):
        cb = nbr(self.m.y, yr)
        copies = []
        for h in range(2):
            cols = pl.ds(pl.multiple_of(cb * 1792 + h * 896, 128), 896)
            copies.append(pltpu.make_async_copy(
                self.got.at[q, yr, h], self.out_hbm.at[pl.ds(q * 32, 32), cols], self.writes.at[q * 8 + yr * 2 + h]))
        return copies

    def finish(self, q, yr):
        for side in range(2):
            self.direct[q, yr, side].wait_recv()
            self.summed[q, yr, side].wait_recv()
        for h in range(2):
            total = (add(self.part[q, yr, 0, h], self.near[q, yr, 0, h])
                     + self.near[q, yr, 1, h].astype(jnp.float32)).astype(jnp.bfloat16)
            if yr:
                self.fin[q, yr, h] = total
            else:
                self.got[q, 0, h] = total
        if yr:
            self.home[q, yr].start()
        else:
            for copy in self.write(q, 0):
                copy.start()


def layer_kernel(
    len_ref, live_ref, q_hbm, qr_hbm, lat_hbm, rope_hbm, new_ref, newr_ref, anc_ref, up_ref, proj_ref,
    out_hbm,
    q_ref, raw_s, qr_ref, lat_ref, rope_ref, tree_s, tree_rope_s, bias_s, turn_s, ctx_s, all_ref, blk_ref,
    hv, act, part, relay, sums, near, fin, got,
    send, recv, local, loads, writes,
):
    factor = score_scale * log2_e
    heads, width, sub = 64, 512, 256
    m = Mover(send, recv)
    plan = gather_plan(m, up_ref, proj_ref, all_ref, blk_ref, local)
    project = Project(m, out_hbm, ctx_s, all_ref, blk_ref, hv, act, part, relay, sums, near, fin, got, writes)

    def begin():
        plan["ready"]()
        project.open(0)
        project.widen(0, 0)

    def side():
        project.widen(0, 1)
        project.widen(0, 3)

    plan.update(open=begin, side=side, across=lambda: project.widen(0, 2))

    def fetch_ropes(r):
        return pltpu.make_async_copy(qr_hbm.at[r], raw_s.at[r], loads.at[6 + r])

    def arrange_ropes(r):
        fetch_ropes(r).wait()
        lane = lax.broadcasted_iota(jnp.int32, (32, 128), 1)
        after = jnp.where(lane == 64, 1.0, 0.0)

        def pair(i, carry):
            both = raw_s[r, :, pl.ds(pl.multiple_of(i * 128, 128), 128)].astype(jnp.float32)
            turn_s[2 * i, :, pl.ds(0, 128)] = jnp.where(lane < 64, both, after)
            turn_s[2 * i + 1, :, pl.ds(0, 128)] = jnp.where(lane < 64, pltpu.roll(both, 64, 1), after)
            return carry

        lax.fori_loop(0, heads // 2, pair, 0, unroll=4)
        for block in range(4):
            turned = jnp.swapaxes(turn_s[:, pl.ds(block * 8, 8), pl.ds(0, 128)], 0, 1)
            qr_ref[r, pl.ds(block * 512, 512), :] = turned.reshape(512, 128).astype(jnp.bfloat16)

    def fetch(r):
        pairs = ((q_hbm.at[r], q_ref.at[r]), (lat_hbm.at[r], lat_ref.at[r]),
                 (rope_hbm.at[r], rope_ref.at[r, pl.ds(0, 64)]))
        return [pltpu.make_async_copy(src, dst, loads.at[r * 3 + i]) for i, (src, dst) in enumerate(pairs)]

    for r in range(2):
        for copy in fetch(r):
            copy.start()
        fetch_ropes(r).start()
    plan["first"]()
    arrange_ropes(0)
    tree_s[...] = jnp.zeros(tree_s.shape, jnp.bfloat16)
    tree_rope_s[...] = jnp.zeros(tree_rope_s.shape, jnp.bfloat16)
    bias_s[...] = jnp.full(bias_s.shape, very_negative, jnp.float32)
    tree_s[:, pl.ds(0, 32), :] = new_ref[...]
    tree_rope_s[:, pl.ds(0, 32), pl.ds(0, 64)] = newr_ref[...]
    bias_s[:, :, pl.ds(0, 32)] = jnp.where(anc_ref[...] > 0, 0.0, very_negative)
    for r in range(2):
        position = lax.broadcasted_iota(jnp.int32, (64, 2048), 1)
        row = lax.broadcasted_iota(jnp.int32, (64, 2048), 0)
        outside = jnp.logical_and(row == 0, position >= len_ref[r])
        rope_ref[r, pl.ds(64, 64), :] = jnp.where(outside, very_negative, 0.0).astype(jnp.bfloat16)

    def step(i, carry):
        for r in range(2):
            @pl.when(i == r * 4)
            def _():
                if r:
                    arrange_ropes(r)
                for copy in fetch(r):
                    copy.wait()

        request = i // 4
        block = lax.rem(i, 4)
        row0 = block * 8

        def queries(part):
            start = pl.multiple_of(row0 * heads + part * sub, sub)
            return q_ref[request, pl.ds(start, sub), :], qr_ref[request, pl.ds(start, sub), :]

        keys = lat_ref[request]
        rope_keys = rope_ref[request]

        def scores(part):
            q, qr = queries(part)
            return (lax.dot_general(q, keys, nt, preferred_element_type=jnp.float32)
                    + jnp.dot(qr, rope_keys, preferred_element_type=jnp.float32))

        def tree_scores(part):
            q, qr = queries(part)
            s = (lax.dot_general(q, tree_s[request], nt, preferred_element_type=jnp.float32)
                 + lax.dot_general(qr, tree_rope_s[request], nt, preferred_element_type=jnp.float32))
            bias = bias_s[request, pl.ds(row0 + part * 4, 4), :]
            return (s.reshape(4, heads, 128) + bias[:, None, :]).reshape(sub, 128)

        both = [(scores(part), tree_scores(part)) for part in range(2)]
        done = []
        for part, (s, t) in enumerate(both):
            top = jnp.maximum(jnp.max(s, axis=1, keepdims=True), jnp.max(t, axis=1, keepdims=True)) * factor
            w = jnp.exp2(s * factor - top)
            v = jnp.exp2(t * factor - top)
            total = jnp.sum(lane_sum(w) + v, axis=1, keepdims=True)
            acc = (jnp.dot(w.astype(jnp.bfloat16), keys, preferred_element_type=jnp.float32)
                   + jnp.dot(v.astype(jnp.bfloat16), tree_s[request], preferred_element_type=jnp.float32))
            ctx = (acc * (1.0 / total)).reshape(4, heads, width)
            alive = row0 + part * 4 + lax.broadcasted_iota(jnp.int32, (4, heads, 1), 0) < live_ref[request]
            done.append(jnp.where(alive, ctx, 0.0))
        ctx = jnp.concatenate(done, axis=0)
        turn_s[:, pl.ds(pl.multiple_of(row0, 8), 8), :] = jnp.swapaxes(ctx, 0, 1)

        @pl.when(i == 3)
        def _():
            ctx_s[...] = turn_s[...].astype(jnp.bfloat16)

        for point, names in schedule.items():
            @pl.when(i == point)
            def _():
                for name in names:
                    plan[name]()
        return carry

    lax.fori_loop(0, 8, step, 0)
    ctx_s[...] = turn_s[...].astype(jnp.bfloat16)
    p = project
    p.open(1)
    plan["block_ready"]()
    p.product(0, 0)
    p.pass_on(0, 0, 2)
    p.widen(1, 0)
    p.pass_sums(0, 0)
    p.pass_on(0, 1, 3)
    p.rest(0)
    p.product(0, 3)
    p.product(0, 1)
    p.widen(1, 1)
    p.widen(1, 3)
    p.pass_sums(0, 3)
    p.pass_sums(0, 1)
    p.widen(1, 2)
    p.finish(0, 0)
    for xr in range(4):
        p.arrived(0, 2, xr)
    p.product(0, 2)
    p.product(1, 0)
    p.finish(0, 3)
    p.finish(0, 1)
    p.pass_on(1, 0, 2)
    p.pass_sums(0, 2)
    p.pass_sums(1, 0)
    p.pass_on(1, 1, 3)
    p.rest(1)
    p.product(1, 3)
    p.product(1, 1)
    p.finish(0, 2)
    p.pass_sums(1, 3)
    p.pass_sums(1, 1)
    p.finish(1, 0)
    for xr in range(4):
        p.arrived(1, 2, xr)
    p.product(1, 2)
    p.finish(1, 3)
    p.finish(1, 1)
    p.pass_sums(1, 2)
    p.finish(1, 2)
    for q in range(2):
        for yr in (1, 3, 2):
            p.home[q, -yr % 4].wait_recv()
            for copy in p.write(q, yr):
                copy.start()
    for copy in m.made:
        copy.wait_send()
    for q in range(2):
        for yr in range(4):
            for copy in p.write(q, yr):
                copy.wait()


def layer(query_lat, query_rope, lat_cache, rope_cache, new_lat, new_rope, cache_len, live_rows, ancestors,
           value_up, out_proj):
    bf = jnp.bfloat16
    queries = query_lat.reshape(2, 2048, 512)
    anywhere = pl.BlockSpec(memory_space=pl.ANY)
    smem, vmem = pl.BlockSpec(memory_space=pltpu.SMEM), pl.BlockSpec(memory_space=pltpu.VMEM)
    copies = 176
    return pl.pallas_call(
        layer_kernel,
        out_shape=jax.ShapeDtypeStruct((64, 7168), bf),
        in_specs=[smem, smem] + [anywhere] * 4 + [vmem] * 3 + [anywhere] * 2,
        out_specs=anywhere,
        scratch_shapes=[
            pltpu.VMEM((2, 2048, 512), bf),
            pltpu.VMEM((2, 32, 4096), bf),
            pltpu.VMEM((2, 2048, 128), bf),
            pltpu.VMEM((2, 2048, 512), bf),
            pltpu.VMEM((2, 128, 2048), bf),
            pltpu.VMEM((2, 128, 512), bf),
            pltpu.VMEM((2, 128, 128), bf),
            pltpu.VMEM((2, 32, 128), jnp.float32),
            pltpu.VMEM((64, 32, 512), jnp.float32),
            pltpu.VMEM((64, 32, 512), bf),
            pltpu.VMEM((16, 4, 512, 128), bf),
            pltpu.VMEM((2, 4, 512, 896), bf),
            pltpu.VMEM((2, 4, 32, 2048), bf),
            pltpu.VMEM((2, 4, 4, 32, 2048), bf),
            pltpu.VMEM((2, 4, 4, 2, 32, 896), bf),
            pltpu.VMEM((2, 4, 2, 32, 896), bf),
            pltpu.VMEM((2, 4, 2, 32, 896), bf),
            pltpu.VMEM((2, 4, 2, 2, 32, 896), bf),
            pltpu.VMEM((2, 4, 2, 32, 896), bf),
            pltpu.VMEM((2, 4, 2, 32, 896), bf),
            pltpu.SemaphoreType.DMA((copies,)), pltpu.SemaphoreType.DMA((copies,)),
            pltpu.SemaphoreType.DMA((3,)), pltpu.SemaphoreType.DMA((8,)), pltpu.SemaphoreType.DMA((16,)),
        ],
        compiler_params=pltpu.CompilerParams(collective_id=0, has_side_effects=True, vmem_limit_bytes=62 * 2**20),
        cost_estimate=pl.CostEstimate(flops=26 * 10**9, bytes_accessed=40 * 2**20, transcendentals=8 * 2**20),
    )(cache_len, live_rows, queries, query_rope, lat_cache, rope_cache, new_lat, new_rope, ancestors, value_up, out_proj)


def per_device(query_lat, query_rope, lat_cache, rope_cache, new_lat, new_rope, cache_len, live_rows, ancestors,
               value_up, out_proj):
    return layer(query_lat, query_rope, lat_cache, rope_cache, new_lat, new_rope, cache_len, live_rows, ancestors,
                 value_up, out_proj)


def solution(mesh):
    both = ("grp", "dp")
    in_specs = (
        P(both, None, None, None), P(both, None, None), P(both, None, None), P(both, None, None),
        P(both, None, None), P(both, None, None), P(both), P(both), P(both, None, None),
        P("dp", None, None), P("dp", None),
    )
    return jax.shard_map(per_device, mesh=mesh, in_specs=in_specs, out_specs=P(both, None), check_vma=False)
```

```python
import functools
import jax
import jax.numpy as jnp
from jax import lax
from jax.experimental import pallas as pl
from jax.experimental.pallas import tpu as pltpu
from jax.sharding import PartitionSpec as P

score_scale = 192.0 ** (-0.5)
log2_e = 1.4426950408889634
very_negative = -1e30
MESH = pl.DeviceIdType.MESH
nt = (((1,), (1,)), ((), ()))


def nbr(base, step):
    return lax.rem(base + step % 4, 4) if step % 4 else base


class Remote:
    def __init__(self, mover, src, dst, step):
        self.mover, self.src, self.dst, self.step = mover, src, dst, step
        self.number = mover.used
        mover.used += 1
        mover.made.append(self)

    def copy(self):
        m = self.mover
        return pltpu.make_async_remote_copy(
            src_ref=self.src(), dst_ref=self.dst(), send_sem=m.send.at[self.number], recv_sem=m.recv.at[self.number],
            device_id=m.device(**self.step), device_id_type=MESH)

    def start(self):
        self.copy().start()
        return self

    def wait_recv(self):
        self.copy().wait_recv()

    def wait_send(self):
        self.copy().wait_send()


class Mover:
    def __init__(self, send, recv):
        self.send, self.recv, self.used, self.made = send, recv, 0, []
        grp, dp = lax.axis_index("grp"), lax.axis_index("dp")
        self.y, self.c = grp // 2, lax.rem(grp, 2)
        self.x, self.z = dp // 4, lax.rem(dp, 4)

    def device(self, x=0, y=0, z=0, c=0):
        cc = lax.rem(self.c + c, 2) if c else self.c
        return (nbr(self.y, y) * 2 + cc, nbr(self.x, x) * 4 + nbr(self.z, z))

    def greet(self, steps):
        barrier = pltpu.get_barrier_semaphore()
        for step in steps:
            pl.semaphore_signal(barrier, inc=1, device_id=self.device(**step), device_id_type=MESH)
        pl.semaphore_wait(barrier, len(steps))

    def later(self, src, dst, **step):
        return Remote(self, src, dst, step)

    def go(self, src, dst, **step):
        return Remote(self, lambda: src, lambda: dst, step).start()


def gather_plan(m, up_ref, proj_ref, all_ref, blk_ref, local):
    x, y, z, c = m.x, m.y, m.z, m.c
    shard = x * 4 + z
    half = pl.ds(pl.multiple_of(c * 256, 256), 256)
    pq = [pl.ds(pl.multiple_of(c * 256 + i * 128, 128), 128) for i in range(2)]
    column = lambda base: pl.ds(base * 4, 4)
    lower = lambda base: pl.ds(base * 4, 2)
    upper = lambda base: pl.ds(base * 4 + 2, 2)
    xl, xr, xo = nbr(x, -1), nbr(x, 1), nbr(x, 2)
    yl, yr, yo = nbr(y, -1), nbr(y, 1), nbr(y, 2)
    zl, zr, zo = nbr(z, -1), nbr(z, 1), nbr(z, 2)

    def at(ref, *index):
        return lambda: ref.at[index]

    def same(ref, *index, **step):
        view = at(ref, *index)
        return m.later(view, view, **step)

    def cols(h):
        return pl.ds(pl.multiple_of(y * 1792 + h * 896, 128), 896)

    own = [lambda: pltpu.make_async_copy(up_ref.at[y, half], all_ref.at[shard, y, half], local.at[0])]
    for h in range(2):
        own.append(lambda h=h: pltpu.make_async_copy(proj_ref.at[:, cols(h)], blk_ref.at[h, z], local.at[1 + h]))

    twins = {}

    def twin(name, ref, *index):
        twins.setdefault(name, []).append(same(ref, *index, c=1))

    zs = [m.later(at(up_ref, y, half), at(all_ref, shard, y, half), z=s) for s in (1, -1, 2)]
    mine = at(proj_ref, slice(None), pl.ds(pl.multiple_of(y * 1792 + c * 896, 128), 896))
    w = [m.later(mine, at(blk_ref, c, z), z=s) for s in (1, -1)]
    wf = [same(blk_ref, c, zl, pl.ds(0, 256), z=1), same(blk_ref, c, zr, pl.ds(256, 256), z=-1)]
    xp = [same(all_ref, column(x), y, pq[0], x=s) for s in (1, -1)]
    yq = [same(all_ref, column(x), y, pq[1], y=s) for s in (1, -1)]
    xpf = [same(all_ref, lower(xl), y, pq[0], x=1), same(all_ref, upper(xr), y, pq[0], x=-1)]
    yqf = [same(all_ref, lower(x), yl, pq[1], y=1), same(all_ref, upper(x), yr, pq[1], y=-1)]
    bases_x, bases_y = (x, xl, xr, xo), (y, yl, yr, yo)
    yp = [[same(all_ref, column(b), y, pq[0], y=s) for s in (1, -1)] for b in bases_x]
    xq = [[same(all_ref, column(x), b, pq[1], x=s) for s in (1, -1)] for b in bases_y]
    ypf = [[same(all_ref, lower(b), yl, pq[0], y=1), same(all_ref, upper(b), yr, pq[0], y=-1)] for b in bases_x]
    xqf = [[same(all_ref, lower(xl), b, pq[1], x=1), same(all_ref, upper(xr), b, pq[1], x=-1)] for b in bases_y]

    twin("spread", all_ref, column(x), y, half)
    for b in (xl, xr):
        twin("near", all_ref, column(b), y, pq[0])
    for b in (yl, yr):
        twin("near", all_ref, column(x), b, pq[1])
    twin("far", all_ref, column(xo), y, pq[0])
    twin("far", all_ref, column(x), yo, pq[1])
    for k in range(4):
        name = "pass%d" % min(k + 1, 3)
        for b in (yl, yr):
            twin(name, all_ref, column(bases_x[k]), b, pq[0])
        for b in (xl, xr):
            twin(name, all_ref, column(b), bases_y[k], pq[1])
        name = "tail%d" % (k // 2)
        twin(name, all_ref, column(bases_x[k]), yo, pq[0])
        twin(name, all_ref, column(xo), bases_y[k], pq[1])
    twin("weights", blk_ref, c, zl)
    twin("weights", blk_ref, c, zr)
    twin("last", blk_ref, c, zo)

    def start(*copies):
        for copy in copies:
            copy.start()

    def got(*copies):
        for copy in copies:
            copy.wait_recv()

    def first():
        for load in own:
            load().start()
        m.greet([dict(x=1), dict(x=-1), dict(x=2), dict(y=1), dict(y=-1), dict(y=2),
                 dict(z=1), dict(z=-1), dict(z=2), dict(c=1)])
        start(*zs)

    def spread():
        own[0]().wait()
        got(*zs)
        start(*w)
        start(*xp, *yq, *yp[0], *xq[0])
        start(*twins["spread"])

    def near():
        got(*xp)
        start(*xpf)
        got(*yq)
        start(*yqf)
        start(*yp[1], *xq[1], *yp[2], *xq[2])
        start(*twins["near"])

    def far():
        got(*xpf, *yqf)
        got(*yp[0], *xq[0])
        start(*ypf[0], *xqf[0], *yp[3], *xq[3])
        start(*twins["far"])

    def pass_on(k):
        def step():
            got(*yp[k], *xq[k])
            start(*ypf[k], *xqf[k])
            start(*twins["pass%d" % k])
        return step

    def weights():
        got(*w)
        start(*wf)
        start(*twins["weights"])

    def tail(name, ks):
        def step():
            for k in ks:
                got(*ypf[k], *xqf[k])
            start(*twins[name])
        return step

    def ready():
        for name, group in twins.items():
            if name not in ("weights", "last"):
                got(*group)

    def block_ready():
        got(*wf)
        start(*twins["last"])
        got(*twins["weights"], *twins["last"])
        for load in own[1:]:
            load().wait()

    return dict(first=first, spread=spread, near=near, far=far, pass1=pass_on(1), pass2=pass_on(2), pass3=pass_on(3),
                weights=weights, ready=ready, block_ready=block_ready, tail0=tail("tail0", (0, 1)), tail1=tail("tail1", (2, 3)))


schedule = {
    0: ["spread"], 1: ["near"], 2: ["far"], 3: ["pass1", "pass2"], 4: ["pass3", "tail0"], 5: ["tail1"],
    6: ["open", "weights"], 7: ["side", "across"],
}


def lane_sum(w):
    parts = [w[:, c * 128:(c + 1) * 128] for c in range(w.shape[1] // 128)]
    while len(parts) > 1:
        parts = [a + b for a, b in zip(parts[::2], parts[1::2])] + (parts[-1:] if len(parts) % 2 else [])
    return parts[0]


def add(a, b):
    return a.astype(jnp.float32) + b.astype(jnp.float32)


class Project:
    def __init__(self, m, out_hbm, turn, up, blk, hv, act, part, relay, sums, near, fin, got, writes):
        self.m, self.out_hbm, self.turn, self.up, self.blk, self.hv, self.act, self.part = (
            m, out_hbm, turn, up, blk, hv, act, part)
        self.relay, self.sums, self.near, self.fin, self.got, self.writes = relay, sums, near, fin, got, writes

        def copy(src, i, dst, j, **step):
            return m.later(lambda: src.at[i], lambda: dst.at[j], **step)

        both, four = range(2), range(4)
        self.swap = {(q, dx): copy(hv, (q, dx), act, (q, 0, -dx % 4), x=dx) for q in both for dx in (1, 3, 2)}
        self.wide = {(q, xr, s): copy(act, (q, 0, xr), act, (q, -s % 4, xr), y=s)
                     for q in both for xr in four for s in (1, -1)}
        self.on = {(q, xr): (copy(act, (q, 3, xr), act, (q, 2, xr), y=1) if xr < 2 else
                             copy(act, (q, 1, xr), act, (q, 2, xr), y=-1)) for q in both for xr in four}
        self.far, self.direct, self.summed, self.home = {}, {}, {}, {}
        for q in both:
            for yr in four:
                for side, xr, way in ((0, 1, 1), (1, 3, -1)):
                    k = (q, yr, side)
                    self.far[k] = copy(part, (q, yr, 2, side), relay, (q, yr, side), x=way)
                    self.direct[k] = copy(part, (q, yr, xr, 1 - side), near, (q, yr, side, 1 - side), x=way)
                    self.summed[k] = copy(sums, (q, yr, side), near, (q, yr, side, side), x=way)
                if yr:
                    self.home[q, yr] = copy(fin, (q, yr), got, (q, -yr % 4), y=yr)

    def values(self, q, dx, target):
        kb = nbr(self.m.x, dx)

        def heads(i, carry):
            h = kb * 16 + i
            v = jnp.dot(self.turn[q, h].astype(jnp.bfloat16), self.up[h // 4, lax.rem(h, 4)], preferred_element_type=jnp.float32)
            target[:, pl.ds(pl.multiple_of(i * 128, 128), 128)] = v.astype(jnp.bfloat16)
            return carry

        lax.fori_loop(0, 16, heads, 0, unroll=8)

    def open(self, q):
        for dx in (1, 3, 2):
            self.values(q, dx, self.hv.at[q, dx])
            self.swap[q, dx].start()
        self.values(q, 0, self.act.at[q, 0, 0])

    def widen(self, q, xr):
        if xr:
            self.swap[q, -xr % 4].wait_recv()
        self.wide[q, xr, 1].start()
        self.wide[q, xr, -1].start()

    def arrived(self, q, yr, xr):
        if yr == 2:
            self.on[q, xr].wait_recv()
        else:
            self.wide[q, xr, 1 if yr == 3 else -1].wait_recv()

    def pass_on(self, q, *xrs):
        for xr in xrs:
            self.arrived(q, 3 if xr < 2 else 1, xr)
            self.on[q, xr].start()

    def rest(self, q):
        for xr in (2, 3):
            self.arrived(q, 3, xr)
        for xr in (0, 1):
            self.arrived(q, 1, xr)

    def product(self, q, yr):
        def columns(h, carry):
            rows = self.act[q, yr].reshape(128, 2048)
            p = jnp.dot(rows, self.blk[h].reshape(2048, 896), preferred_element_type=jnp.float32).astype(jnp.bfloat16)
            for xr in range(4):
                self.part[q, yr, xr, h] = p[xr * 32:(xr + 1) * 32]
            return carry

        lax.fori_loop(0, 2, columns, 0)
        for side in range(2):
            self.far[q, yr, side].start()
        for side in range(2):
            self.direct[q, yr, side].start()

    def pass_sums(self, q, yr):
        for side, xr in ((0, 1), (1, 3)):
            self.far[q, yr, side].wait_recv()
            self.sums[q, yr, side] = add(self.part[q, yr, xr, side], self.relay[q, yr, side]).astype(jnp.bfloat16)
            self.summed[q, yr, side].start()

    def write(self, q, yr):
        cb = nbr(self.m.y, yr)
        copies = []
        for h in range(2):
            cols = pl.ds(pl.multiple_of(cb * 1792 + h * 896, 128), 896)
            copies.append(pltpu.make_async_copy(
                self.got.at[q, yr, h], self.out_hbm.at[pl.ds(q * 32, 32), cols], self.writes.at[q * 8 + yr * 2 + h]))
        return copies

    def finish(self, q, yr):
        for side in range(2):
            self.direct[q, yr, side].wait_recv()
            self.summed[q, yr, side].wait_recv()
        for h in range(2):
            total = (add(self.part[q, yr, 0, h], self.near[q, yr, 0, h])
                     + self.near[q, yr, 1, h].astype(jnp.float32)).astype(jnp.bfloat16)
            if yr:
                self.fin[q, yr, h] = total
            else:
                self.got[q, 0, h] = total
        if yr:
            self.home[q, yr].start()
        else:
            for copy in self.write(q, 0):
                copy.start()


def layer_kernel(
    len_ref, live_ref, q_hbm, qr_hbm, lat_hbm, rope_hbm, new_ref, newr_ref, anc_ref, up_ref, proj_ref,
    out_hbm,
    q_ref, raw_s, qr_ref, lat_ref, rope_ref, tree_s, tree_rope_s, bias_s, turn_s, all_ref, blk_ref,
    hv, act, part, relay, sums, near, fin, got,
    send, recv, local, loads, writes,
):
    factor = score_scale * log2_e
    heads, width, sub = 64, 512, 256
    m = Mover(send, recv)
    plan = gather_plan(m, up_ref, proj_ref, all_ref, blk_ref, local)
    project = Project(m, out_hbm, turn_s, all_ref, blk_ref, hv, act, part, relay, sums, near, fin, got, writes)

    def begin():
        plan["ready"]()
        project.open(0)
        project.widen(0, 0)

    def side():
        project.widen(0, 1)
        project.widen(0, 3)

    plan.update(open=begin, side=side, across=lambda: project.widen(0, 2))

    def fetch_ropes(r):
        return pltpu.make_async_copy(qr_hbm.at[r], raw_s.at[r], loads.at[6 + r])

    def arrange_ropes(r):
        fetch_ropes(r).wait()
        lane = lax.broadcasted_iota(jnp.int32, (32, 128), 1)
        after = jnp.where(lane == 64, 1.0, 0.0)

        def pair(i, carry):
            both = raw_s[r, :, pl.ds(pl.multiple_of(i * 128, 128), 128)].astype(jnp.float32)
            turn_s[r, 2 * i, :, pl.ds(0, 128)] = jnp.where(lane < 64, both, after)
            turn_s[r, 2 * i + 1, :, pl.ds(0, 128)] = jnp.where(lane < 64, pltpu.roll(both, 64, 1), after)
            return carry

        lax.fori_loop(0, heads // 2, pair, 0, unroll=4)
        for block in range(4):
            turned = jnp.swapaxes(turn_s[r, :, pl.ds(block * 8, 8), pl.ds(0, 128)], 0, 1)
            qr_ref[r, pl.ds(block * 512, 512), :] = turned.reshape(512, 128).astype(jnp.bfloat16)

    def fetch(r):
        pairs = ((q_hbm.at[r], q_ref.at[r]), (lat_hbm.at[r], lat_ref.at[r]),
                 (rope_hbm.at[r], rope_ref.at[r, pl.ds(0, 64)]))
        return [pltpu.make_async_copy(src, dst, loads.at[r * 3 + i]) for i, (src, dst) in enumerate(pairs)]

    for r in range(2):
        for copy in fetch(r):
            copy.start()
        fetch_ropes(r).start()
    plan["first"]()
    arrange_ropes(0)
    tree_s[...] = jnp.zeros(tree_s.shape, jnp.bfloat16)
    tree_rope_s[...] = jnp.zeros(tree_rope_s.shape, jnp.bfloat16)
    bias_s[...] = jnp.full(bias_s.shape, very_negative, jnp.float32)
    tree_s[:, pl.ds(0, 32), :] = new_ref[...]
    tree_rope_s[:, pl.ds(0, 32), pl.ds(0, 64)] = newr_ref[...]
    bias_s[:, :, pl.ds(0, 32)] = jnp.where(anc_ref[...] > 0, 0.0, very_negative)
    for r in range(2):
        position = lax.broadcasted_iota(jnp.int32, (64, 2048), 1)
        row = lax.broadcasted_iota(jnp.int32, (64, 2048), 0)
        outside = jnp.logical_and(row == 0, position >= len_ref[r])
        rope_ref[r, pl.ds(64, 64), :] = jnp.where(outside, very_negative, 0.0).astype(jnp.bfloat16)

    def step(i, carry):
        for r in range(2):
            @pl.when(i == r * 4)
            def _():
                if r:
                    arrange_ropes(r)
                for copy in fetch(r):
                    copy.wait()

        request = i // 4
        block = lax.rem(i, 4)
        row0 = block * 8

        def queries(part):
            start = pl.multiple_of(row0 * heads + part * sub, sub)
            return q_ref[request, pl.ds(start, sub), :], qr_ref[request, pl.ds(start, sub), :]

        keys = lat_ref[request]
        rope_keys = rope_ref[request]

        def scores(part):
            q, qr = queries(part)
            return (lax.dot_general(q, keys, nt, preferred_element_type=jnp.float32)
                    + jnp.dot(qr, rope_keys, preferred_element_type=jnp.float32))

        def tree_scores(part):
            q, qr = queries(part)
            s = (lax.dot_general(q, tree_s[request], nt, preferred_element_type=jnp.float32)
                 + lax.dot_general(qr, tree_rope_s[request], nt, preferred_element_type=jnp.float32))
            bias = bias_s[request, pl.ds(row0 + part * 4, 4), :]
            return (s.reshape(4, heads, 128) + bias[:, None, :]).reshape(sub, 128)

        both = [(scores(part), tree_scores(part)) for part in range(2)]
        done = []
        for part, (s, t) in enumerate(both):
            top = jnp.maximum(jnp.max(s, axis=1, keepdims=True), jnp.max(t, axis=1, keepdims=True)) * factor
            w = jnp.exp2(s * factor - top)
            v = jnp.exp2(t * factor - top)
            total = jnp.sum(lane_sum(w) + v, axis=1, keepdims=True)
            acc = (jnp.dot(w.astype(jnp.bfloat16), keys, preferred_element_type=jnp.float32)
                   + jnp.dot(v.astype(jnp.bfloat16), tree_s[request], preferred_element_type=jnp.float32))
            ctx = (acc * (1.0 / total)).reshape(4, heads, width)
            alive = row0 + part * 4 + lax.broadcasted_iota(jnp.int32, (4, heads, 1), 0) < live_ref[request]
            done.append(jnp.where(alive, ctx, 0.0))
        ctx = jnp.concatenate(done, axis=0)
        turn_s[request, :, pl.ds(pl.multiple_of(row0, 8), 8), :] = jnp.swapaxes(ctx, 0, 1)

        for point, names in schedule.items():
            @pl.when(i == point)
            def _():
                for name in names:
                    plan[name]()
        return carry

    lax.fori_loop(0, 8, step, 0)
    p = project
    p.open(1)
    plan["block_ready"]()
    p.product(0, 0)
    p.pass_on(0, 0, 2)
    p.widen(1, 0)
    p.pass_sums(0, 0)
    p.pass_on(0, 1, 3)
    p.rest(0)
    p.product(0, 3)
    p.product(0, 1)
    p.widen(1, 1)
    p.widen(1, 3)
    p.pass_sums(0, 3)
    p.pass_sums(0, 1)
    p.widen(1, 2)
    p.finish(0, 0)
    for xr in range(4):
        p.arrived(0, 2, xr)
    p.product(0, 2)
    p.product(1, 0)
    p.finish(0, 3)
    p.finish(0, 1)
    p.pass_on(1, 0, 2)
    p.pass_sums(0, 2)
    p.pass_sums(1, 0)
    p.pass_on(1, 1, 3)
    p.rest(1)
    p.product(1, 3)
    p.product(1, 1)
    p.finish(0, 2)
    p.pass_sums(1, 3)
    p.pass_sums(1, 1)
    p.finish(1, 0)
    for xr in range(4):
        p.arrived(1, 2, xr)
    p.product(1, 2)
    p.finish(1, 3)
    p.finish(1, 1)
    p.pass_sums(1, 2)
    p.finish(1, 2)
    for q in range(2):
        for yr in (1, 3, 2):
            p.home[q, -yr % 4].wait_recv()
            for copy in p.write(q, yr):
                copy.start()
    for copy in m.made:
        copy.wait_send()
    for q in range(2):
        for yr in range(4):
            for copy in p.write(q, yr):
                copy.wait()


def layer(query_lat, query_rope, lat_cache, rope_cache, new_lat, new_rope, cache_len, live_rows, ancestors,
           value_up, out_proj):
    bf = jnp.bfloat16
    queries = query_lat.reshape(2, 2048, 512)
    anywhere = pl.BlockSpec(memory_space=pl.ANY)
    smem, vmem = pl.BlockSpec(memory_space=pltpu.SMEM), pl.BlockSpec(memory_space=pltpu.VMEM)
    copies = 176
    return pl.pallas_call(
        layer_kernel,
        out_shape=jax.ShapeDtypeStruct((64, 7168), bf),
        in_specs=[smem, smem] + [anywhere] * 4 + [vmem] * 3 + [anywhere] * 2,
        out_specs=anywhere,
        scratch_shapes=[
            pltpu.VMEM((2, 2048, 512), bf),
            pltpu.VMEM((2, 32, 4096), bf),
            pltpu.VMEM((2, 2048, 128), bf),
            pltpu.VMEM((2, 2048, 512), bf),
            pltpu.VMEM((2, 128, 2048), bf),
            pltpu.VMEM((2, 128, 512), bf),
            pltpu.VMEM((2, 128, 128), bf),
            pltpu.VMEM((2, 32, 128), jnp.float32),
            pltpu.VMEM((2, 64, 32, 512), jnp.float32),
            pltpu.VMEM((16, 4, 512, 128), bf),
            pltpu.VMEM((2, 4, 512, 896), bf),
            pltpu.VMEM((2, 4, 32, 2048), bf),
            pltpu.VMEM((2, 4, 4, 32, 2048), bf),
            pltpu.VMEM((2, 4, 4, 2, 32, 896), bf),
            pltpu.VMEM((2, 4, 2, 32, 896), bf),
            pltpu.VMEM((2, 4, 2, 32, 896), bf),
            pltpu.VMEM((2, 4, 2, 2, 32, 896), bf),
            pltpu.VMEM((2, 4, 2, 32, 896), bf),
            pltpu.VMEM((2, 4, 2, 32, 896), bf),
            pltpu.SemaphoreType.DMA((copies,)), pltpu.SemaphoreType.DMA((copies,)),
            pltpu.SemaphoreType.DMA((3,)), pltpu.SemaphoreType.DMA((8,)), pltpu.SemaphoreType.DMA((16,)),
        ],
        compiler_params=pltpu.CompilerParams(collective_id=0, has_side_effects=True, vmem_limit_bytes=62 * 2**20),
        cost_estimate=pl.CostEstimate(flops=26 * 10**9, bytes_accessed=40 * 2**20, transcendentals=8 * 2**20),
    )(cache_len, live_rows, queries, query_rope, lat_cache, rope_cache, new_lat, new_rope, ancestors, value_up, out_proj)


def per_device(query_lat, query_rope, lat_cache, rope_cache, new_lat, new_rope, cache_len, live_rows, ancestors,
               value_up, out_proj):
    return layer(query_lat, query_rope, lat_cache, rope_cache, new_lat, new_rope, cache_len, live_rows, ancestors,
                 value_up, out_proj)


def solution(mesh):
    both = ("grp", "dp")
    in_specs = (
        P(both, None, None, None), P(both, None, None), P(both, None, None), P(both, None, None),
        P(both, None, None), P(both, None, None), P(both), P(both), P(both, None, None),
        P("dp", None, None), P("dp", None),
    )
    return jax.shard_map(per_device, mesh=mesh, in_specs=in_specs, out_specs=P(both, None), check_vma=False)
```
